512 devices in a mesh: gx: 32 (over x, y), gy: 16 (over z, core).
Axes of the slice: x: 4, y: 8, z: 8, core: 2. Of those that a mesh axis runs over, the one named last changes fastest.
Arguments:
- intensity: float32 [4, 4096, 2048], P(None, 'gx', 'gy'), may hold values from -6 to 6
- reach_along_x: float32 [4, 2048], P(None, 'gy'), may hold values from 8 to 16384
- reach_along_y: float32 [4, 4096], P(None, 'gx'), may hold values from 8 to 8192
Outputs:
- smoothed: float32 [4, 4096, 2048], P(None, 'gx', 'gy')
The draws below stay inside these ranges and needn't reach their ends.
All inputs are finite; a program needn't handle non-finite values.
Results may differ from the reference program's by a relative error of at most 0.00011.
Values sent between devices are 32-bit elements; how exact they have to be, the bound alone decides.
No kernel may reach another device: no remote copies, remote signals or barrier semaphores. Data moves between devices by JAX's collectives and lax.ppermute only.
A program may use at most 128 MiB of HBM per device.

```python
import math
import jax
import jax.numpy as jnp
from jax import lax

Z = 4
NX = 4096
NY = 2048


def level_of(rng, dims, split, least, largest):
    loudness = 1.0
    for axis_at, shards_of in split:
        draws = jax.random.uniform(jax.random.fold_in(jax.random.fold_in(rng, 6), axis_at), (shards_of,), jnp.float32, least / len(split), largest / len(split))
        loudness = loudness * jnp.repeat(jnp.exp(draws), dims[axis_at] // shards_of).reshape((-1,) + (1,) * (len(dims) - 1 - axis_at))
    return loudness


def centred(rng, extent, width, most, pieces=(), kind=jnp.bfloat16):
    values = width * jax.random.normal(rng, extent, jnp.float32)
    if pieces:
        values = values * level_of(rng, extent, pieces, -0.22, 0.18)
    return jnp.clip(values, -most, most).astype(kind)


def setup_inputs(seed: int = 0) -> dict:
    keys = jax.random.split(jax.random.key(seed), 4)
    return {
        "intensity": centred(keys[0], (Z, NX, NY), 1.0, 6.0, ((1, 32), (2, 16)), jnp.float32),
        "reach_along_x": jnp.clip(jnp.exp(math.log(16384.0) - 7.624619 * jax.random.uniform(keys[1], (Z, NY), jnp.float32) ** level_of(keys[1], (Z, NY), ((1, 16),), -0.2, 0.2)), 8.0, 16384.0),
        "reach_along_y": jnp.clip(jnp.exp(math.log(8192.0) - 6.931472 * jax.random.uniform(keys[2], (Z, NX), jnp.float32) ** level_of(keys[2], (Z, NX), ((1, 32),), -0.2, 0.2)), 8.0, 8192.0),
    }


edge_slope = 3.0


def decay_map(gradient, reach):
    return jnp.exp(-(1.0 + edge_slope * jnp.abs(gradient)) / reach)


def pole_list(decay):
    poles = [decay]
    for level in range(3):
        poles.append(poles[-1] * poles[-1])
    return poles


def first_order(values, pole, reverse):
    def advance(carried, inputs):
        source, weight = inputs
        output = weight * carried + (1.0 - weight) * source
        return output, output

    zeroes = jnp.zeros(values.shape[1:], jnp.float32)
    _, result = lax.scan(advance, zeroes, (values, pole), reverse=reverse)
    return result


def cascade(values, decay):
    poles = pole_list(decay)
    for pole in poles:
        values = first_order(values, pole, False)
    for pole in poles:
        values = first_order(values, pole, True)
    return values


def reference(intensity, reach_along_x, reach_along_y):
    padded = jnp.pad(intensity, ((0, 0), (1, 1), (1, 1)))
    gradient_x = 0.5 * (padded[:, 2:, 1:-1] - padded[:, :-2, 1:-1])
    gradient_y = 0.5 * (padded[:, 1:-1, 2:] - padded[:, 1:-1, :-2])
    decay_x = decay_map(gradient_x, reach_along_x[:, None, :])
    decay_y = decay_map(gradient_y, reach_along_y[:, :, None])
    lines_x = jnp.transpose(intensity, (1, 0, 2))
    decay_lines = jnp.transpose(decay_x, (1, 0, 2))
    across_x = cascade(lines_x, decay_lines)
    lines_y = jnp.transpose(across_x, (2, 1, 0))
    decay_lines_y = jnp.transpose(decay_y, (2, 0, 1))
    across_y = cascade(lines_y, decay_lines_y)
    return jnp.transpose(across_y, (1, 2, 0))
```

```python
import functools

import jax
import jax.numpy as jnp
from jax import lax
from jax.experimental import pallas as pl
from jax.experimental.pallas import tpu as pltpu
from jax.sharding import PartitionSpec as P

edge_slope = 3.0

LOWER = [(k, j) for k in range(4) for j in range(k + 1)]
BELOW = [(k, j) for k in range(4) for j in range(k)]
FULL = [(k, j) for k in range(4) for j in range(4)]
VALUES = 37

params = pltpu.CompilerParams(vmem_limit_bytes=48 * 1024 * 1024)
MATRICES = 29
SLOTS = 48
APART = 9


def unpack_matrices(get):
    A, B = {}, {}
    for n, kj in enumerate(BELOW):
        A[kj], B[kj] = get(1 + n), get(7 + n)
    power = get(0)
    for k in range(4):
        A[k, k] = B[k, k] = power
        power = power * power
    return A, B, {kj: get(13 + n) for n, kj in enumerate(FULL)}


def pack_matrices(matrices):
    A, B, C = matrices
    return [A[0, 0]] + [A[kj] for kj in BELOW] + [B[kj] for kj in BELOW] + [C[kj] for kj in FULL]


def unpack(get):
    A, B, C = unpack_matrices(get)
    vectors = [get(MATRICES + n) for n in range(8)]
    return A, vectors[:4], B, C, vectors[4:]


def pack(block):
    A, u, B, C, w = block
    return pack_matrices((A, B, C)) + list(u) + list(w)


def total(terms):
    terms = list(terms)
    while len(terms) > 1:
        terms = [a + b for a, b in zip(terms[::2], terms[1::2])] + terms[len(terms) - len(terms) % 2 :]
    return terms[0]


def lower_times(M, x):
    return [total([M[k, j] * x[j] for j in range(k + 1)]) for k in range(4)]


def full_times(M, x):
    return [total([M[k, j] * x[j] for j in range(4)]) for k in range(4)]


def plus(x, y):
    return [a + b for a, b in zip(x, y)]


def lower_product(M, N):
    return {(k, j): total([M[k, i] * N[i, j] for i in range(j, k + 1)]) for k, j in LOWER}


def compose_matrices(left, right):
    A1, B1, C1 = left
    A2, B2, C2 = right
    A = lower_product(A2, A1)
    B = lower_product(B1, B2)
    CA = {(k, j): total([C2[k, i] * A1[i, j] for i in range(j, 4)]) for k, j in FULL}
    C = {(k, j): total([B1[k, i] * CA[i, j] for i in range(k + 1)]) + C1[k, j] for k, j in FULL}
    return A, B, C


def compose_vectors(B1, A2, C2, left, right):
    u1, w1 = left
    u2, w2 = right
    u = plus(lower_times(A2, u1), u2)
    w = plus(lower_times(B1, plus(full_times(C2, u1), w2)), w1)
    return u, w


def compose(left, right):
    A1, u1, B1, C1, w1 = left
    A2, u2, B2, C2, w2 = right
    A, B, C = compose_matrices((A1, B1, C1), (A2, B2, C2))
    u, w = compose_vectors(B1, A2, C2, (u1, w1), (u2, w2))
    return A, u, B, C, w


def forward_out(block, f):
    A, u = block[:2]
    return [total([A[k, j] * f[j] for j in range(k + 1)] + [u[k]]) for k in range(4)]


def backward_out(block, f, b):
    B, C, w = block[2:]
    return [total([B[k, j] * b[j] for j in range(k + 1)] + [C[k, j] * f[j] for j in range(4)] + [w[k]]) for k in range(4)]


def poles_of(d):
    p = [d]
    for _ in range(3):
        p.append(p[-1] * p[-1])
    return p, [1.0 - x for x in p]


STEPS, UNROLL = 64, 8
PITCH = 65
padded = (8 * PITCH, 128)


def loop(body, carry, reverse=False):
    def some(n, carry):
        for k in range(UNROLL):
            at = n * UNROLL + k
            carry = body(STEPS - 1 - at if reverse else at, carry)
        return carry

    return lax.fori_loop(0, STEPS // UNROLL, some, carry)


def rows(s):
    return pl.ds(s, 8, stride=PITCH)


def decay_block(v, inverse):
    at = lax.broadcasted_iota(jnp.int32, v.shape, 0)
    n = v.shape[0]
    gradient = 0.5 * (pltpu.roll(v, n - 1, 0) - pltpu.roll(v, 1, 0))
    d = jnp.exp((1.0 + edge_slope * jnp.abs(gradient)) * inverse)
    return jnp.where((at == 0) | (at == n - 1), 1.0, d)


def cascade_lower(p, q, M):
    M = dict(M)
    for j in range(4):
        M[j, j] = p[j] * M[j, j]
        for k in range(j + 1, 4):
            M[k, j] = p[k] * M[k, j] + q[k] * M[k - 1, j]
    return M


def cascade_source(p, q, x, source):
    x = list(x)
    for k in range(4):
        x[k] = p[k] * x[k] + q[k] * (source if k == 0 else x[k - 1])
    return x


def before_step(p, q, B):
    new, inner = {}, []
    for k in range(4):
        carried = B[k, k]
        new[k, k] = p[k] * carried
        for j in reversed(range(k)):
            carried = B[k, j] + q[j + 1] * carried
            new[k, j] = p[j] * carried
        inner.append(q[0] * carried)
    return new, inner


def half_maps(v_ref, d_ref):
    one, zero = jnp.ones((8, 128), jnp.float32), jnp.zeros((8, 128), jnp.float32)

    def step(s, carry):
        A, u, B, C, w = carry
        A, B = dict(zip(LOWER, A)), dict(zip(LOWER, B))
        p, q = poles_of(d_ref[rows(s), :])
        u = cascade_source(p, q, u, v_ref[rows(s), :])
        A = cascade_lower(p, q, A)
        B, inner = before_step(p, q, B)
        C = [c + inner[k] * A[3, j] for c, (k, j) in zip(C, FULL)]
        w = [x + y * u[3] for x, y in zip(w, inner)]
        return [A[kj] for kj in LOWER], u, [B[kj] for kj in LOWER], C, w

    start = [one if k == j else zero for k, j in LOWER]
    A, u, B, C, w = loop(step, (start, [zero] * 4, start, [zero] * 16, [zero] * 4))
    return dict(zip(LOWER, A)), u, dict(zip(LOWER, B)), dict(zip(FULL, C)), w


def after(part):
    if isinstance(part, dict):
        return {key: pltpu.roll(x, 7, 0) for key, x in part.items()}
    return [pltpu.roll(x, 7, 0) for x in part]


def planes():
    return [slice(z * 128, (z + 1) * 128) for z in range(4)]


def place(i):
    return pl.ds(i // STEPS * PITCH + i % STEPS, 4, stride=2 * PITCH)


def spread(ref, z, block):
    for h in range(2):
        at = (2 * z + h) * PITCH
        ref[at : at + STEPS, :] = block[h * STEPS : (h + 1) * STEPS]


def gather(ref, z):
    at = 2 * z * PITCH
    return jnp.concatenate([ref[at : at + STEPS, :], ref[at + PITCH : at + PITCH + STEPS, :]], axis=0)


def swap(x, groups):
    row, lane = (lax.broadcasted_iota(jnp.int32, x.shape, axis) for axis in range(2))
    width = 128 // groups
    t = 1
    while t < groups:
        lower, right = (row // t) % 2 == 1, (lane // (width * t)) % 2 == 1
        up = pltpu.roll(pltpu.roll(x, 8 - t, 0), width * t, 1)
        down = pltpu.roll(pltpu.roll(x, t, 0), 128 - width * t, 1)
        x = jnp.where(lower == right, x, jnp.where(lower, down, up))
        t *= 2
    return x


def summarise(v_ref, source_ref, reach_ref, d_ref, half_ref, chunks_ref, pair_ref):
    for z, here in enumerate(planes()):
        spread(d_ref, z, decay_block(v_ref[here, :], -1.0 / reach_ref[z : z + 1, :]))
    block = half_maps(source_ref, d_ref)
    for n, value in enumerate(pack(block)):
        half_ref[n] = value
    for n, value in enumerate(pack(compose(block, tuple(after(part) for part in block)))):
        pair_ref[n * APART : n * APART + 8, :] = value
    ends = [v_ref[pl.ds(i, 4, stride=128), :] for i in (0, 1, 126, 127)] + [source_ref[place(0), :], source_ref[place(127), :], reach_ref[...]]
    for n, value in enumerate(ends):
        pair_ref[pl.ds((37 + n) * APART, 4, stride=2), :] = value
    for n in range(44, SLOTS):
        pair_ref[n * APART : n * APART + 8, :] = jnp.zeros((8, 128), jnp.float32)
    per_plane = chunks_ref.shape[0] // 4
    groups = per_plane
    for z in range(4):
        chunks = slice(z * per_plane, (z + 1) * per_plane)
        for n in range(0, SLOTS, 8):
            x = swap(pair_ref[pl.ds(n * APART + 2 * z, 8, stride=APART), :], groups)
            for a in range(8 // groups):
                chunks_ref[chunks, n // groups + a, :] = x[a * groups : (a + 1) * groups]


def finish(v_ref, half_ref, state_ref, d_ref, c_ref, out_ref, wide_ref):
    groups = state_ref.shape[0] // 4
    count = 8 // groups
    for z in range(4):
        chunks = slice(z * groups, (z + 1) * groups)
        x = swap(jnp.concatenate([state_ref[chunks, a, :] for a in range(count)], axis=0), groups)
        wide_ref[pl.ds(2 * z, 8, stride=APART), :] = x
        wide_ref[pl.ds(2 * z + 1, 8, stride=APART), :] = x
        x = swap(jnp.concatenate([state_ref[chunks, count, :]] * count, axis=0), groups)
        first, last = 2 * z * PITCH, (2 * z + 1) * PITCH + STEPS - 1
        d_ref[first : first + 1, :] = x[0:1]
        d_ref[last : last + 1, :] = x[1:2]
    f = [wide_ref[k * APART : k * APART + 8, :] for k in range(4)]
    b = [wide_ref[k * APART : k * APART + 8, :] for k in range(4, 8)]
    block = unpack(lambda n: half_ref[n])
    second = lax.broadcasted_iota(jnp.int32, (8, 128), 0) % 2 == 1
    p, q = poles_of(d_ref[rows(0), :])
    f_middle = [pltpu.roll(x, 1, 0) for x in forward_out(block, cascade_source(p, q, f, v_ref[rows(0), :]))]
    p, q = poles_of(d_ref[rows(STEPS - 1), :])
    f_last = cascade_source(p, q, forward_out(block, f_middle), v_ref[rows(STEPS - 1), :])
    b_middle = [pltpu.roll(x, 7, 0) for x in backward_out(block, f_middle, cascade_source(p, q, b, f_last[3]))]
    f = [jnp.where(second, x, y) for x, y in zip(f_middle, f)]
    b = [jnp.where(second, y, x) for x, y in zip(b_middle, b)]

    def forward(s, f):
        p, q = poles_of(d_ref[rows(s), :])
        f = cascade_source(p, q, f, v_ref[rows(s), :])
        c_ref[s] = f[3]
        return f

    loop(forward, f)

    def backward(s, b):
        p, q = poles_of(d_ref[rows(s), :])
        b = cascade_source(p, q, b, c_ref[s])
        out_ref[rows(s), :] = b[3]
        return b

    loop(backward, b, reverse=True)


def x_first(arguments_ref, vt_ref, y_reach_ref, source_ref, d_ref, half_ref, chunks_ref, reach_ref, pair_ref):
    for z, here in enumerate(planes()):
        vt_ref[here, :] = arguments_ref[here, :].T
        spread(source_ref, z, arguments_ref[here, :])
    reach_ref[...] = arguments_ref[512:516, :]
    y_reach_ref[...] = arguments_ref[516:520, :]
    summarise(arguments_ref, source_ref, reach_ref, d_ref, half_ref, chunks_ref, pair_ref)


def x_second_y_first(
    vt_ref, reach_ref, source_ref, dx_ref, xhalf_ref, state_ref,
    t_ref, d_ref, half_ref, chunks_ref,
    ends_ref, c_ref, across_ref, wide_ref, pair_ref,
):
    ends_ref[...] = dx_ref[...]
    finish(source_ref, xhalf_ref, state_ref, ends_ref, c_ref, across_ref, wide_ref)
    for z in range(4):
        spread(t_ref, z, gather(across_ref, z).T)
    summarise(vt_ref, t_ref, reach_ref, d_ref, half_ref, chunks_ref, pair_ref)


def y_second(t_ref, d_ref, half_ref, state_ref, out_ref, ends_ref, c_ref, done_ref, wide_ref):
    ends_ref[...] = d_ref[...]
    finish(t_ref, half_ref, state_ref, ends_ref, c_ref, done_ref, wide_ref)
    for z, here in enumerate(planes()):
        out_ref[here, :] = gather(done_ref, z).T


def with_ends(block, first, last, source_first, source_last):
    A, u, B, C, w = block
    one, zero = jnp.ones_like(first), jnp.zeros_like(first)
    identity = {(k, j): one if k == j else zero for k, j in LOWER}
    p, q = poles_of(last)
    A, u = cascade_lower(p, q, A), cascade_source(p, q, u, source_last)
    inner = lower_times(B, cascade_source(p, q, [zero] * 4, one))
    B = lower_product(B, cascade_lower(p, q, identity))
    C = {(k, j): C[k, j] + inner[k] * A[3, j] for k, j in FULL}
    w = [x + y * u[3] for x, y in zip(w, inner)]
    p, q = poles_of(first)
    T, t = cascade_lower(p, q, identity), cascade_source(p, q, [zero] * 4, source_first)
    w = plus(w, full_times(C, t))
    u = plus(u, lower_times(A, t))
    A = lower_product(A, T)
    C = {(k, j): total([C[k, i] * T[i, j] for i in range(j, 4)]) for k, j in FULL}
    columns = [cascade_source(p, q, [C[k, j] for k in range(4)], T[3, j]) for j in range(4)]
    C = {(k, j): columns[j][k] for k, j in FULL}
    w = cascade_source(p, q, w, t[3])
    B = cascade_lower(p, q, B)
    return A, u, B, C, w


def line_scan(groups, blocks_ref, state_ref, map_ref, f_ref, b_ref):
    count, width = blocks_ref.shape[0], 128 // groups
    eights = count // 8
    row = lax.broadcasted_iota(jnp.int32, (8, 128), 0)
    group = lax.broadcasted_iota(jnp.int32, (8, 128), 1) // width

    def moved(x, by):
        by = by * width % 128
        return pltpu.roll(x, by, 1) if by else x

    def value(n):
        parts = [moved(blocks_ref[8 * g : 8 * g + 8, n // groups, :], g - n % groups) for g in range(eights)]
        x = parts[0]
        for g in range(1, eights):
            x = jnp.where(group == g, parts[g], x)
        return x

    v = [value(37 + n) for n in range(4)]
    below = pltpu.roll(v[3], 1, 0)
    below = jnp.where(row == 0, jnp.where(group == 0, 0.0, moved(below, 1)), below)
    above = pltpu.roll(v[0], 7, 0)
    above = jnp.where(row == 7, jnp.where(group == eights - 1, 0.0, moved(above, -1)), above)
    inverse = -1.0 / value(43)
    first, last = (
        jnp.exp((1.0 + edge_slope * jnp.abs(gradient)) * inverse) for gradient in (0.5 * (v[1] - below), 0.5 * (above - v[2]))
    )
    block = with_ends(unpack(value), first, last, value(41), value(42))
    for n, x in enumerate(pack(block)):
        map_ref[n] = x

    def block_at(m):
        return unpack(lambda n: map_ref[n, m : m + 1, :])

    for reach in (1, 2, 4):
        other = tuple(
            {key: pltpu.roll(x, 8 - reach, 0) for key, x in part.items()} if isinstance(part, dict) else [pltpu.roll(x, 8 - reach, 0) for x in part]
            for part in block
        )
        block = compose(block, other)
    joined = unpack(lambda n, values=pack(block): values[n][0:1])

    here = group[0:1]
    zero = [jnp.zeros((1, 128), jnp.float32)] * 4
    f = zero
    for g in range(1, eights):
        through = [moved(x, 1) for x in forward_out(joined, f)]
        f = [jnp.where(here == g, x, y) for x, y in zip(through, f)]
    b = zero
    for g in reversed(range(eights - 1)):
        through = [moved(x, -1) for x in backward_out(joined, f, b)]
        b = [jnp.where(here == g, x, y) for x, y in zip(through, b)]

    inside = []
    for m in range(8):
        for k in range(4):
            f_ref[k, m : m + 1, :] = f[k]
        inside.append(f)
        f = forward_out(block_at(m), f)
    for m in reversed(range(8)):
        for k in range(4):
            b_ref[k, m : m + 1, :] = b[k]
        b = backward_out(block_at(m), inside[m], b)

    back = [f_ref[k] for k in range(4)] + [b_ref[k] for k in range(4)] + [first, last]
    for g in range(eights):
        some = slice(8 * g, 8 * g + 8)
        for start in range(0, 10, groups):
            x = moved(back[start], -g)
            for n in range(1, min(groups, 10 - start)):
                x = jnp.where(group == n, moved(back[start + n], n - g), x)
            state_ref[some, start // groups, :] = x
    for r in range(-(-10 // groups), state_ref.shape[1]):
        state_ref[:, r, :] = jnp.zeros((count, 128), jnp.float32)


f32 = lambda *shape: jax.ShapeDtypeStruct(shape, jnp.float32)
vmem = lambda *shape: pltpu.VMEM(shape, jnp.float32)
plane = (512, 128)


def call(kernel, out_shape, scratch, *operands):
    return pl.pallas_call(kernel, out_shape=out_shape, scratch_shapes=scratch, compiler_params=params)(*operands)


def states(chunks, axis):
    size = lax.axis_size(axis)
    groups = size // 4
    chunks = lax.all_to_all(chunks, axis, 0, 0, tiled=True)
    scratch = [vmem(37, 8, 128), vmem(4, 8, 128), vmem(4, 8, 128)]
    entering = call(functools.partial(line_scan, groups), f32(size, 16 // groups, 128), scratch, chunks)
    return lax.all_to_all(entering, axis, 0, 0, tiled=True)


def per_device(intensity, reach_along_x, reach_along_y):
    def maps(axis):
        size = lax.axis_size(axis)
        return [f32(*padded), f32(37, 8, 128), f32(size, 256 // size, 128)]

    work = [vmem(SLOTS * APART, 128)]
    ending = [vmem(*padded), vmem(STEPS, 8, 128), vmem(*padded), vmem(8 * APART, 128)]
    vt, y_reach, source, dx, x_half, x_chunks = call(
        x_first, [f32(*plane), f32(4, 128), f32(*padded)] + maps("gx"), [vmem(4, 128)] + work,
        jnp.concatenate([intensity.reshape(plane), reach_along_x, reach_along_y]),
    )
    x_states = states(x_chunks, "gx")
    t, dy, y_half, y_chunks = call(
        x_second_y_first, [f32(*padded)] + maps("gy"), ending + work, vt, y_reach, source, dx, x_half, x_states
    )
    y_states = states(y_chunks, "gy")
    out = call(y_second, f32(*plane), ending, t, dy, y_half, y_states)
    return out.reshape(4, 128, 128)


def solution(mesh):
    return jax.shard_map(
        per_device,
        mesh=mesh,
        in_specs=(P(None, "gx", "gy"), P(None, "gy"), P(None, "gx")),
        out_specs=P(None, "gx", "gy"),
        check_vma=False,
    )
```

```python
import functools

import jax
import jax.numpy as jnp
from jax import lax
from jax.experimental import pallas as pl
from jax.experimental.pallas import tpu as pltpu
from jax.sharding import PartitionSpec as P

edge_slope = 3.0

LOWER = [(k, j) for k in range(4) for j in range(k + 1)]
BELOW = [(k, j) for k in range(4) for j in range(k)]
FULL = [(k, j) for k in range(4) for j in range(4)]
VALUES = 37

params = pltpu.CompilerParams(vmem_limit_bytes=48 * 1024 * 1024)
MATRICES = 29
SLOTS = 48
APART = 9


def unpack_matrices(get):
    A, B = {}, {}
    for n, kj in enumerate(BELOW):
        A[kj], B[kj] = get(1 + n), get(7 + n)
    power = get(0)
    for k in range(4):
        A[k, k] = B[k, k] = power
        power = power * power
    return A, B, {kj: get(13 + n) for n, kj in enumerate(FULL)}


def pack_matrices(matrices):
    A, B, C = matrices
    return [A[0, 0]] + [A[kj] for kj in BELOW] + [B[kj] for kj in BELOW] + [C[kj] for kj in FULL]


def unpack(get):
    A, B, C = unpack_matrices(get)
    vectors = [get(MATRICES + n) for n in range(8)]
    return A, vectors[:4], B, C, vectors[4:]


def pack(block):
    A, u, B, C, w = block
    return pack_matrices((A, B, C)) + list(u) + list(w)


def total(terms):
    terms = list(terms)
    while len(terms) > 1:
        terms = [a + b for a, b in zip(terms[::2], terms[1::2])] + terms[len(terms) - len(terms) % 2 :]
    return terms[0]


def lower_times(M, x):
    return [total([M[k, j] * x[j] for j in range(k + 1)]) for k in range(4)]


def full_times(M, x):
    return [total([M[k, j] * x[j] for j in range(4)]) for k in range(4)]


def plus(x, y):
    return [a + b for a, b in zip(x, y)]


def lower_product(M, N):
    return {(k, j): total([M[k, i] * N[i, j] for i in range(j, k + 1)]) for k, j in LOWER}


def compose_matrices(left, right):
    A1, B1, C1 = left
    A2, B2, C2 = right
    A = lower_product(A2, A1)
    B = lower_product(B1, B2)
    CA = {(k, j): total([C2[k, i] * A1[i, j] for i in range(j, 4)]) for k, j in FULL}
    C = {(k, j): total([B1[k, i] * CA[i, j] for i in range(k + 1)]) + C1[k, j] for k, j in FULL}
    return A, B, C


def compose_vectors(B1, A2, C2, left, right):
    u1, w1 = left
    u2, w2 = right
    u = plus(lower_times(A2, u1), u2)
    w = plus(lower_times(B1, plus(full_times(C2, u1), w2)), w1)
    return u, w


def compose(left, right):
    A1, u1, B1, C1, w1 = left
    A2, u2, B2, C2, w2 = right
    A, B, C = compose_matrices((A1, B1, C1), (A2, B2, C2))
    u, w = compose_vectors(B1, A2, C2, (u1, w1), (u2, w2))
    return A, u, B, C, w


def forward_out(block, f):
    A, u = block[:2]
    return [total([A[k, j] * f[j] for j in range(k + 1)] + [u[k]]) for k in range(4)]


def backward_out(block, f, b):
    B, C, w = block[2:]
    return [total([B[k, j] * b[j] for j in range(k + 1)] + [C[k, j] * f[j] for j in range(4)] + [w[k]]) for k in range(4)]


def poles_of(d):
    p = [d]
    for _ in range(3):
        p.append(p[-1] * p[-1])
    return p, [1.0 - x for x in p]


STEPS, UNROLL = 64, 16
PITCH = 65
padded = (8 * PITCH, 128)


def loop(body, carry, reverse=False):
    def some(n, carry):
        for k in range(UNROLL):
            at = n * UNROLL + k
            carry = body(STEPS - 1 - at if reverse else at, carry)
        return carry

    return lax.fori_loop(0, STEPS // UNROLL, some, carry)


def rows(s):
    return pl.ds(s, 8, stride=PITCH)


def decay_block(v, inverse):
    at = lax.broadcasted_iota(jnp.int32, v.shape, 0)
    n = v.shape[0]
    gradient = 0.5 * (pltpu.roll(v, n - 1, 0) - pltpu.roll(v, 1, 0))
    d = jnp.exp((1.0 + edge_slope * jnp.abs(gradient)) * inverse)
    return jnp.where((at == 0) | (at == n - 1), 1.0, d)


def cascade_lower(p, q, M):
    M = dict(M)
    for j in range(4):
        M[j, j] = p[j] * M[j, j]
        for k in range(j + 1, 4):
            M[k, j] = p[k] * M[k, j] + q[k] * M[k - 1, j]
    return M


def cascade_source(p, q, x, source):
    x = list(x)
    for k in range(4):
        x[k] = p[k] * x[k] + q[k] * (source if k == 0 else x[k - 1])
    return x


def before_step(p, q, B):
    new, inner = {}, []
    for k in range(4):
        carried = B[k, k]
        new[k, k] = p[k] * carried
        for j in reversed(range(k)):
            carried = B[k, j] + q[j + 1] * carried
            new[k, j] = p[j] * carried
        inner.append(q[0] * carried)
    return new, inner


def half_maps(v_ref, d_ref):
    one, zero = jnp.ones((8, 128), jnp.float32), jnp.zeros((8, 128), jnp.float32)

    def step(s, carry):
        A, u, B, C, w = carry
        A, B = dict(zip(LOWER, A)), dict(zip(LOWER, B))
        p, q = poles_of(d_ref[rows(s), :])
        u = cascade_source(p, q, u, v_ref[rows(s), :])
        A = cascade_lower(p, q, A)
        B, inner = before_step(p, q, B)
        C = [c + inner[k] * A[3, j] for c, (k, j) in zip(C, FULL)]
        w = [x + y * u[3] for x, y in zip(w, inner)]
        return [A[kj] for kj in LOWER], u, [B[kj] for kj in LOWER], C, w

    start = [one if k == j else zero for k, j in LOWER]
    A, u, B, C, w = loop(step, (start, [zero] * 4, start, [zero] * 16, [zero] * 4))
    return dict(zip(LOWER, A)), u, dict(zip(LOWER, B)), dict(zip(FULL, C)), w


def after(part):
    if isinstance(part, dict):
        return {key: pltpu.roll(x, 7, 0) for key, x in part.items()}
    return [pltpu.roll(x, 7, 0) for x in part]


def planes():
    return [slice(z * 128, (z + 1) * 128) for z in range(4)]


def place(i):
    return pl.ds(i // STEPS * PITCH + i % STEPS, 4, stride=2 * PITCH)


def spread(ref, z, block):
    for h in range(2):
        at = (2 * z + h) * PITCH
        ref[at : at + STEPS, :] = block[h * STEPS : (h + 1) * STEPS]


def gather(ref, z):
    at = 2 * z * PITCH
    return jnp.concatenate([ref[at : at + STEPS, :], ref[at + PITCH : at + PITCH + STEPS, :]], axis=0)


def swap(x, groups):
    row, lane = (lax.broadcasted_iota(jnp.int32, x.shape, axis) for axis in range(2))
    width = 128 // groups
    t = 1
    while t < groups:
        lower, right = (row // t) % 2 == 1, (lane // (width * t)) % 2 == 1
        up = pltpu.roll(pltpu.roll(x, 8 - t, 0), width * t, 1)
        down = pltpu.roll(pltpu.roll(x, t, 0), 128 - width * t, 1)
        x = jnp.where(lower == right, x, jnp.where(lower, down, up))
        t *= 2
    return x


def summarise(v_ref, source_ref, reach_ref, d_ref, half_ref, chunks_ref, pair_ref):
    for z, here in enumerate(planes()):
        spread(d_ref, z, decay_block(v_ref[here, :], -1.0 / reach_ref[z : z + 1, :]))
    block = half_maps(source_ref, d_ref)
    for n, value in enumerate(pack(block)):
        half_ref[n] = value
    for n, value in enumerate(pack(compose(block, tuple(after(part) for part in block)))):
        pair_ref[n * APART : n * APART + 8, :] = value
    ends = [v_ref[pl.ds(i, 4, stride=128), :] for i in (0, 1, 126, 127)] + [source_ref[place(0), :], source_ref[place(127), :], reach_ref[...]]
    for n, value in enumerate(ends):
        pair_ref[pl.ds((37 + n) * APART, 4, stride=2), :] = value
    for n in range(44, SLOTS):
        pair_ref[n * APART : n * APART + 8, :] = jnp.zeros((8, 128), jnp.float32)
    if chunks_ref.shape[1] == SLOTS:
        row = lax.broadcasted_iota(jnp.int32, (8, 128), 0)
        for z in range(4):
            for n in range(0, SLOTS, 8):
                x = pair_ref[pl.ds(n * APART + 2 * z, 8, stride=APART), :]
                for at in range(z, chunks_ref.shape[0], 4):
                    chunks_ref[at, n : n + 8, :] = x if n != 40 else jnp.where(row == 4, float(at // 4), x)
        return
    per_plane = chunks_ref.shape[0] // 4
    groups = per_plane
    for z in range(4):
        chunks = slice(z * per_plane, (z + 1) * per_plane)
        for n in range(0, SLOTS, 8):
            x = swap(pair_ref[pl.ds(n * APART + 2 * z, 8, stride=APART), :], groups)
            for a in range(8 // groups):
                chunks_ref[chunks, n // groups + a, :] = x[a * groups : (a + 1) * groups]


def finish(v_ref, half_ref, state_ref, d_ref, c_ref, out_ref, wide_ref):
    groups = state_ref.shape[0] // 4
    for z in range(4):
        chunks = slice(z * groups, (z + 1) * groups)
        if groups == 1:
            x, ends = state_ref[z, 0:8, :], state_ref[z, 8:16, :]
        else:
            count = 8 // groups
            x = swap(jnp.concatenate([state_ref[chunks, a, :] for a in range(count)], axis=0), groups)
            ends = swap(jnp.concatenate([state_ref[chunks, count, :]] * count, axis=0), groups)
        wide_ref[pl.ds(2 * z, 8, stride=APART), :] = x
        wide_ref[pl.ds(2 * z + 1, 8, stride=APART), :] = x
        first, last = 2 * z * PITCH, (2 * z + 1) * PITCH + STEPS - 1
        d_ref[first : first + 1, :] = ends[0:1]
        d_ref[last : last + 1, :] = ends[1:2]
    f = [wide_ref[k * APART : k * APART + 8, :] for k in range(4)]
    b = [wide_ref[k * APART : k * APART + 8, :] for k in range(4, 8)]
    block = unpack(lambda n: half_ref[n])
    second = lax.broadcasted_iota(jnp.int32, (8, 128), 0) % 2 == 1
    p, q = poles_of(d_ref[rows(0), :])
    f_middle = [pltpu.roll(x, 1, 0) for x in forward_out(block, cascade_source(p, q, f, v_ref[rows(0), :]))]
    p, q = poles_of(d_ref[rows(STEPS - 1), :])
    f_last = cascade_source(p, q, forward_out(block, f_middle), v_ref[rows(STEPS - 1), :])
    b_middle = [pltpu.roll(x, 7, 0) for x in backward_out(block, f_middle, cascade_source(p, q, b, f_last[3]))]
    f = [jnp.where(second, x, y) for x, y in zip(f_middle, f)]
    b = [jnp.where(second, y, x) for x, y in zip(b_middle, b)]

    def forward(s, f):
        p, q = poles_of(d_ref[rows(s), :])
        f = cascade_source(p, q, f, v_ref[rows(s), :])
        c_ref[s] = f[3]
        return f

    loop(forward, f)

    def backward(s, b):
        p, q = poles_of(d_ref[rows(s), :])
        b = cascade_source(p, q, b, c_ref[s])
        out_ref[rows(s), :] = b[3]
        return b

    loop(backward, b, reverse=True)


def x_first(arguments_ref, vt_ref, y_reach_ref, source_ref, d_ref, half_ref, chunks_ref, reach_ref, pair_ref):
    for z, here in enumerate(planes()):
        vt_ref[here, :] = arguments_ref[here, :].T
        spread(source_ref, z, arguments_ref[here, :])
    reach_ref[...] = arguments_ref[512:516, :]
    y_reach_ref[...] = arguments_ref[516:520, :]
    summarise(arguments_ref, source_ref, reach_ref, d_ref, half_ref, chunks_ref, pair_ref)


def x_second_y_first(
    vt_ref, reach_ref, source_ref, dx_ref, xhalf_ref, state_ref,
    t_ref, d_ref, half_ref, chunks_ref,
    ends_ref, c_ref, across_ref, wide_ref, pair_ref,
):
    ends_ref[...] = dx_ref[...]
    finish(source_ref, xhalf_ref, state_ref, ends_ref, c_ref, across_ref, wide_ref)
    for z in range(4):
        spread(t_ref, z, gather(across_ref, z).T)
    summarise(vt_ref, t_ref, reach_ref, d_ref, half_ref, chunks_ref, pair_ref)


def y_second(t_ref, d_ref, half_ref, state_ref, out_ref, ends_ref, c_ref, done_ref, wide_ref):
    ends_ref[...] = d_ref[...]
    finish(t_ref, half_ref, state_ref, ends_ref, c_ref, done_ref, wide_ref)
    for z, here in enumerate(planes()):
        out_ref[here, :] = gather(done_ref, z).T


def with_ends(block, first, last, source_first, source_last):
    A, u, B, C, w = block
    one, zero = jnp.ones_like(first), jnp.zeros_like(first)
    identity = {(k, j): one if k == j else zero for k, j in LOWER}
    p, q = poles_of(last)
    A, u = cascade_lower(p, q, A), cascade_source(p, q, u, source_last)
    inner = lower_times(B, cascade_source(p, q, [zero] * 4, one))
    B = lower_product(B, cascade_lower(p, q, identity))
    C = {(k, j): C[k, j] + inner[k] * A[3, j] for k, j in FULL}
    w = [x + y * u[3] for x, y in zip(w, inner)]
    p, q = poles_of(first)
    T, t = cascade_lower(p, q, identity), cascade_source(p, q, [zero] * 4, source_first)
    w = plus(w, full_times(C, t))
    u = plus(u, lower_times(A, t))
    A = lower_product(A, T)
    C = {(k, j): total([C[k, i] * T[i, j] for i in range(j, 4)]) for k, j in FULL}
    columns = [cascade_source(p, q, [C[k, j] for k in range(4)], T[3, j]) for j in range(4)]
    C = {(k, j): columns[j][k] for k, j in FULL}
    w = cascade_source(p, q, w, t[3])
    B = cascade_lower(p, q, B)
    return A, u, B, C, w


def line_scan(groups, blocks_ref, state_ref, map_ref, f_ref, b_ref):
    count, width = blocks_ref.shape[0], 128 // groups
    eights = count // 8
    row = lax.broadcasted_iota(jnp.int32, (8, 128), 0)
    group = lax.broadcasted_iota(jnp.int32, (8, 128), 1) // width

    def moved(x, by):
        by = by * width % 128
        return pltpu.roll(x, by, 1) if by else x

    def value(n):
        parts = [moved(blocks_ref[8 * g : 8 * g + 8, n // groups, :], g - n % groups) for g in range(eights)]
        x = parts[0]
        for g in range(1, eights):
            x = jnp.where(group == g, parts[g], x)
        return x

    v = [value(37 + n) for n in range(4)]
    below = pltpu.roll(v[3], 1, 0)
    below = jnp.where(row == 0, jnp.where(group == 0, 0.0, moved(below, 1)), below)
    above = pltpu.roll(v[0], 7, 0)
    above = jnp.where(row == 7, jnp.where(group == eights - 1, 0.0, moved(above, -1)), above)
    inverse = -1.0 / value(43)
    first, last = (
        jnp.exp((1.0 + edge_slope * jnp.abs(gradient)) * inverse) for gradient in (0.5 * (v[1] - below), 0.5 * (above - v[2]))
    )
    block = with_ends(unpack(value), first, last, value(41), value(42))
    for n, x in enumerate(pack(block)):
        map_ref[n] = x

    def block_at(m):
        return unpack(lambda n: map_ref[n, m : m + 1, :])

    for reach in (1, 2, 4):
        other = tuple(
            {key: pltpu.roll(x, 8 - reach, 0) for key, x in part.items()} if isinstance(part, dict) else [pltpu.roll(x, 8 - reach, 0) for x in part]
            for part in block
        )
        block = compose(block, other)
    joined = unpack(lambda n, values=pack(block): values[n][0:1])

    here = group[0:1]
    zero = [jnp.zeros((1, 128), jnp.float32)] * 4
    f = zero
    for g in range(1, eights):
        through = [moved(x, 1) for x in forward_out(joined, f)]
        f = [jnp.where(here == g, x, y) for x, y in zip(through, f)]
    b = zero
    for g in reversed(range(eights - 1)):
        through = [moved(x, -1) for x in backward_out(joined, f, b)]
        b = [jnp.where(here == g, x, y) for x, y in zip(through, b)]

    inside = []
    for m in range(8):
        for k in range(4):
            f_ref[k, m : m + 1, :] = f[k]
        inside.append(f)
        f = forward_out(block_at(m), f)
    for m in reversed(range(8)):
        for k in range(4):
            b_ref[k, m : m + 1, :] = b[k]
        b = backward_out(block_at(m), inside[m], b)

    back = [f_ref[k] for k in range(4)] + [b_ref[k] for k in range(4)] + [first, last]
    for g in range(eights):
        some = slice(8 * g, 8 * g + 8)
        for start in range(0, 10, groups):
            x = moved(back[start], -g)
            for n in range(1, min(groups, 10 - start)):
                x = jnp.where(group == n, moved(back[start + n], n - g), x)
            state_ref[some, start // groups, :] = x
    for r in range(-(-10 // groups), state_ref.shape[1]):
        state_ref[:, r, :] = jnp.zeros((count, 128), jnp.float32)


def plane_scan(blocks_ref, state_ref, map_ref, f_ref, b_ref):
    count = blocks_ref.shape[0]
    row = lax.broadcasted_iota(jnp.int32, (count, 128), 0)
    value = lambda n: blocks_ref[:, n, :]
    v = [value(37 + n) for n in range(4)]
    below = jnp.where(row == 0, 0.0, pltpu.roll(v[3], 1, 0))
    above = jnp.where(row == count - 1, 0.0, pltpu.roll(v[0], count - 1, 0))
    inverse = -1.0 / value(43)
    for n, gradient in enumerate((0.5 * (v[1] - below), 0.5 * (above - v[2]))):
        map_ref[37 + n] = jnp.exp((1.0 + edge_slope * jnp.abs(gradient)) * inverse)
    for start in range(0, count, 8):
        some = slice(start, start + 8)
        block = unpack(lambda n: blocks_ref[some, n, :])
        block = with_ends(block, map_ref[37, some, :], map_ref[38, some, :], blocks_ref[some, 41, :], blocks_ref[some, 42, :])
        for n, x in enumerate(pack(block)):
            map_ref[n, some, :] = x

    def block_at(m):
        return unpack(lambda n: map_ref[n, m : m + 1, :])

    f = [jnp.zeros((1, 128), jnp.float32)] * 4
    for m in range(count):
        for k in range(4):
            f_ref[k, m : m + 1, :] = f[k]
        f = forward_out(block_at(m), f)
    b = [jnp.zeros((1, 128), jnp.float32)] * 4
    for m in reversed(range(count)):
        for k in range(4):
            b_ref[k, m : m + 1, :] = b[k]
        b = backward_out(block_at(m), [f_ref[k, m : m + 1, :] for k in range(4)], b)

    here = jnp.broadcast_to(blocks_ref[0, 44:45, :], (4, 128))

    def mine(at):
        x = at(0)
        for g in range(1, count // 4):
            x = jnp.where(here == float(g), at(g), x)
        return x

    for k in range(4):
        state_ref[:, k, :] = mine(lambda g: f_ref[k, 4 * g : 4 * g + 4, :])
        state_ref[:, 4 + k, :] = mine(lambda g: b_ref[k, 4 * g : 4 * g + 4, :])
    for n in range(2):
        state_ref[:, 8 + n, :] = mine(lambda g: map_ref[37 + n, 4 * g : 4 * g + 4, :])
    for n in range(10, 16):
        state_ref[:, n, :] = jnp.zeros((4, 128), jnp.float32)


f32 = lambda *shape: jax.ShapeDtypeStruct(shape, jnp.float32)
vmem = lambda *shape: pltpu.VMEM(shape, jnp.float32)
plane = (512, 128)


def call(kernel, out_shape, scratch, *operands):
    return pl.pallas_call(kernel, out_shape=out_shape, scratch_shapes=scratch, compiler_params=params)(*operands)


def states(chunks, axis):
    size = lax.axis_size(axis)
    groups = size // 4
    chunks = lax.all_to_all(chunks, axis, 0, 0, tiled=True)
    scratch = [vmem(37, 8, 128), vmem(4, 8, 128), vmem(4, 8, 128)]
    entering = call(functools.partial(line_scan, groups), f32(size, 16 // groups, 128), scratch, chunks)
    return lax.all_to_all(entering, axis, 0, 0, tiled=True)


def states_by_planes(chunks, axis):
    size = lax.axis_size(axis)
    blocks = lax.all_to_all(chunks, axis, 0, 0, tiled=True)
    entering = call(plane_scan, f32(4, 16, 128), [vmem(39, size, 128), vmem(4, size, 128), vmem(4, size, 128)], blocks)
    fours = [[4 * g + i for i in range(4)] for g in range(size // 4)]
    return lax.all_to_all(entering, axis, 0, 0, axis_index_groups=fours, tiled=True)


def per_device(intensity, reach_along_x, reach_along_y):
    def maps(axis):
        size = lax.axis_size(axis)
        return [f32(*padded), f32(37, 8, 128), f32(size, SLOTS if axis == "gy" else 256 // size, 128)]

    work = [vmem(SLOTS * APART, 128)]
    ending = [vmem(*padded), vmem(STEPS, 8, 128), vmem(*padded), vmem(8 * APART, 128)]
    vt, y_reach, source, dx, x_half, x_chunks = call(
        x_first, [f32(*plane), f32(4, 128), f32(*padded)] + maps("gx"), [vmem(4, 128)] + work,
        jnp.concatenate([intensity.reshape(plane), reach_along_x, reach_along_y]),
    )
    x_states = states(x_chunks, "gx")
    t, dy, y_half, y_chunks = call(
        x_second_y_first, [f32(*padded)] + maps("gy"), ending + work, vt, y_reach, source, dx, x_half, x_states
    )
    y_states = states_by_planes(y_chunks, "gy")
    out = call(y_second, f32(*plane), ending, t, dy, y_half, y_states)
    return out.reshape(4, 128, 128)


def solution(mesh):
    return jax.shard_map(
        per_device,
        mesh=mesh,
        in_specs=(P(None, "gx", "gy"), P(None, "gy"), P(None, "gx")),
        out_specs=P(None, "gx", "gy"),
        check_vma=False,
    )
```

```python
import functools

import jax
import jax.numpy as jnp
from jax import lax
from jax.experimental import pallas as pl
from jax.experimental.pallas import tpu as pltpu
from jax.sharding import PartitionSpec as P

edge_slope = 3.0

LOWER = [(k, j) for k in range(4) for j in range(k + 1)]
BELOW = [(k, j) for k in range(4) for j in range(k)]
FULL = [(k, j) for k in range(4) for j in range(4)]
VALUES = 37

params = pltpu.CompilerParams(vmem_limit_bytes=48 * 1024 * 1024)
MATRICES = 29
SLOTS = 48
APART = 9


def unpack_matrices(get):
    A, B = {}, {}
    for n, kj in enumerate(BELOW):
        A[kj], B[kj] = get(1 + n), get(7 + n)
    power = get(0)
    for k in range(4):
        A[k, k] = B[k, k] = power
        power = power * power
    return A, B, {kj: get(13 + n) for n, kj in enumerate(FULL)}


def pack_matrices(matrices):
    A, B, C = matrices
    return [A[0, 0]] + [A[kj] for kj in BELOW] + [B[kj] for kj in BELOW] + [C[kj] for kj in FULL]


def unpack(get):
    A, B, C = unpack_matrices(get)
    vectors = [get(MATRICES + n) for n in range(8)]
    return A, vectors[:4], B, C, vectors[4:]


def pack(block):
    A, u, B, C, w = block
    return pack_matrices((A, B, C)) + list(u) + list(w)


def total(terms):
    terms = list(terms)
    while len(terms) > 1:
        terms = [a + b for a, b in zip(terms[::2], terms[1::2])] + terms[len(terms) - len(terms) % 2 :]
    return terms[0]


def lower_times(M, x):
    return [total([M[k, j] * x[j] for j in range(k + 1)]) for k in range(4)]


def full_times(M, x):
    return [total([M[k, j] * x[j] for j in range(4)]) for k in range(4)]


def plus(x, y):
    return [a + b for a, b in zip(x, y)]


def lower_product(M, N):
    return {(k, j): total([M[k, i] * N[i, j] for i in range(j, k + 1)]) for k, j in LOWER}


def compose_matrices(left, right):
    A1, B1, C1 = left
    A2, B2, C2 = right
    A = lower_product(A2, A1)
    B = lower_product(B1, B2)
    CA = {(k, j): total([C2[k, i] * A1[i, j] for i in range(j, 4)]) for k, j in FULL}
    C = {(k, j): total([B1[k, i] * CA[i, j] for i in range(k + 1)]) + C1[k, j] for k, j in FULL}
    return A, B, C


def compose_vectors(B1, A2, C2, left, right):
    u1, w1 = left
    u2, w2 = right
    u = plus(lower_times(A2, u1), u2)
    w = plus(lower_times(B1, plus(full_times(C2, u1), w2)), w1)
    return u, w


def compose(left, right):
    A1, u1, B1, C1, w1 = left
    A2, u2, B2, C2, w2 = right
    A, B, C = compose_matrices((A1, B1, C1), (A2, B2, C2))
    u, w = compose_vectors(B1, A2, C2, (u1, w1), (u2, w2))
    return A, u, B, C, w


def forward_out(block, f):
    A, u = block[:2]
    return [total([A[k, j] * f[j] for j in range(k + 1)] + [u[k]]) for k in range(4)]


def backward_out(block, f, b):
    B, C, w = block[2:]
    return [total([B[k, j] * b[j] for j in range(k + 1)] + [C[k, j] * f[j] for j in range(4)] + [w[k]]) for k in range(4)]


def poles_of(d):
    p = [d]
    for _ in range(3):
        p.append(p[-1] * p[-1])
    return p, [1.0 - x for x in p]


STEPS, UNROLL = 64, 16
PITCH = 65
padded = (8 * PITCH, 128)


def loop(body, carry, reverse=False):
    def some(n, carry):
        for k in range(UNROLL):
            at = n * UNROLL + k
            carry = body(STEPS - 1 - at if reverse else at, carry)
        return carry

    return lax.fori_loop(0, STEPS // UNROLL, some, carry)


def rows(s):
    return pl.ds(s, 8, stride=PITCH)


def decay_block(v, inverse):
    at = lax.broadcasted_iota(jnp.int32, v.shape, 0)
    n = v.shape[0]
    gradient = 0.5 * (pltpu.roll(v, n - 1, 0) - pltpu.roll(v, 1, 0))
    d = jnp.exp((1.0 + edge_slope * jnp.abs(gradient)) * inverse)
    return jnp.where((at == 0) | (at == n - 1), 1.0, d)


def cascade_lower(p, q, M):
    M = dict(M)
    for j in range(4):
        M[j, j] = p[j] * M[j, j]
        for k in range(j + 1, 4):
            M[k, j] = p[k] * M[k, j] + q[k] * M[k - 1, j]
    return M


def cascade_source(p, q, x, source):
    x = list(x)
    for k in range(4):
        x[k] = p[k] * x[k] + q[k] * (source if k == 0 else x[k - 1])
    return x


def before_step(p, q, B):
    new, inner = {}, []
    for k in range(4):
        carried = B[k, k]
        new[k, k] = p[k] * carried
        for j in reversed(range(k)):
            carried = B[k, j] + q[j + 1] * carried
            new[k, j] = p[j] * carried
        inner.append(q[0] * carried)
    return new, inner


def half_maps(v_ref, d_ref):
    one, zero = jnp.ones((8, 128), jnp.float32), jnp.zeros((8, 128), jnp.float32)

    def step(s, carry):
        A, u, B, C, w = carry
        A, B = dict(zip(LOWER, A)), dict(zip(LOWER, B))
        p, q = poles_of(d_ref[rows(s), :])
        u = cascade_source(p, q, u, v_ref[rows(s), :])
        A = cascade_lower(p, q, A)
        B, inner = before_step(p, q, B)
        C = [c + inner[k] * A[3, j] for c, (k, j) in zip(C, FULL)]
        w = [x + y * u[3] for x, y in zip(w, inner)]
        return [A[kj] for kj in LOWER], u, [B[kj] for kj in LOWER], C, w

    start = [one if k == j else zero for k, j in LOWER]
    A, u, B, C, w = loop(step, (start, [zero] * 4, start, [zero] * 16, [zero] * 4))
    return dict(zip(LOWER, A)), u, dict(zip(LOWER, B)), dict(zip(FULL, C)), w


def after(part):
    if isinstance(part, dict):
        return {key: pltpu.roll(x, 7, 0) for key, x in part.items()}
    return [pltpu.roll(x, 7, 0) for x in part]


def planes():
    return [slice(z * 128, (z + 1) * 128) for z in range(4)]


def place(i):
    return pl.ds(i // STEPS * PITCH + i % STEPS, 4, stride=2 * PITCH)


def spread(ref, z, block):
    for h in range(2):
        at = (2 * z + h) * PITCH
        ref[at : at + STEPS, :] = block[h * STEPS : (h + 1) * STEPS]


def gather(ref, z):
    at = 2 * z * PITCH
    return jnp.concatenate([ref[at : at + STEPS, :], ref[at + PITCH : at + PITCH + STEPS, :]], axis=0)


def swap(x, groups):
    row, lane = (lax.broadcasted_iota(jnp.int32, x.shape, axis) for axis in range(2))
    width = 128 // groups
    t = 1
    while t < groups:
        lower, right = (row // t) % 2 == 1, (lane // (width * t)) % 2 == 1
        up = pltpu.roll(pltpu.roll(x, 8 - t, 0), width * t, 1)
        down = pltpu.roll(pltpu.roll(x, t, 0), 128 - width * t, 1)
        x = jnp.where(lower == right, x, jnp.where(lower, down, up))
        t *= 2
    return x


def summarise(v_ref, source_ref, reach_ref, d_ref, half_ref, chunks_ref, pair_ref):
    for z, here in enumerate(planes()):
        spread(d_ref, z, decay_block(v_ref[here, :], -1.0 / reach_ref[z : z + 1, :]))
    block = half_maps(source_ref, d_ref)
    for n, value in enumerate(pack(block)):
        half_ref[n] = value
    for n, value in enumerate(pack(compose(block, tuple(after(part) for part in block)))):
        pair_ref[n * APART : n * APART + 8, :] = value
    ends = [v_ref[pl.ds(i, 4, stride=128), :] for i in (0, 1, 126, 127)] + [source_ref[place(0), :], source_ref[place(127), :], reach_ref[...]]
    for n, value in enumerate(ends):
        pair_ref[pl.ds((37 + n) * APART, 4, stride=2), :] = value
    for n in range(44, SLOTS):
        pair_ref[n * APART : n * APART + 8, :] = jnp.zeros((8, 128), jnp.float32)
    if chunks_ref.shape[2] == 4:
        for z in range(4):
            for n in range(0, 44, 4):
                x = pair_ref[pl.ds(n * APART + 2 * z, 4, stride=APART), :]
                for at in range(z, chunks_ref.shape[0], 4):
                    chunks_ref[at, n // 4] = x
        return
    per_plane = chunks_ref.shape[0] // 4
    groups = per_plane
    for z in range(4):
        chunks = slice(z * per_plane, (z + 1) * per_plane)
        for n in range(0, SLOTS, 8):
            x = swap(pair_ref[pl.ds(n * APART + 2 * z, 8, stride=APART), :], groups)
            for a in range(8 // groups):
                r = n // groups + a
                chunks_ref[chunks, r // 2, r % 2, :] = x[a * groups : (a + 1) * groups]


def finish(v_ref, half_ref, state_ref, d_ref, c_ref, out_ref, wide_ref):
    groups = state_ref.shape[0] // 4
    for z in range(4):
        chunks = slice(z * groups, (z + 1) * groups)
        if groups == 1:
            x, ends = state_ref[z, 0:8, :], state_ref[z, 8:16, :]
        else:
            count = 8 // groups
            x = swap(jnp.concatenate([state_ref[chunks, a, :] for a in range(count)], axis=0), groups)
            ends = swap(jnp.concatenate([state_ref[chunks, count, :]] * count, axis=0), groups)
        wide_ref[pl.ds(2 * z, 8, stride=APART), :] = x
        wide_ref[pl.ds(2 * z + 1, 8, stride=APART), :] = x
        first, last = 2 * z * PITCH, (2 * z + 1) * PITCH + STEPS - 1
        d_ref[first : first + 1, :] = ends[0:1]
        d_ref[last : last + 1, :] = ends[1:2]
    f = [wide_ref[k * APART : k * APART + 8, :] for k in range(4)]
    b = [wide_ref[k * APART : k * APART + 8, :] for k in range(4, 8)]
    block = unpack(lambda n: half_ref[n])
    second = lax.broadcasted_iota(jnp.int32, (8, 128), 0) % 2 == 1
    p, q = poles_of(d_ref[rows(0), :])
    f_middle = [pltpu.roll(x, 1, 0) for x in forward_out(block, cascade_source(p, q, f, v_ref[rows(0), :]))]
    p, q = poles_of(d_ref[rows(STEPS - 1), :])
    f_last = cascade_source(p, q, forward_out(block, f_middle), v_ref[rows(STEPS - 1), :])
    b_middle = [pltpu.roll(x, 7, 0) for x in backward_out(block, f_middle, cascade_source(p, q, b, f_last[3]))]
    f = [jnp.where(second, x, y) for x, y in zip(f_middle, f)]
    b = [jnp.where(second, y, x) for x, y in zip(b_middle, b)]

    def forward(s, f):
        p, q = poles_of(d_ref[rows(s), :])
        f = cascade_source(p, q, f, v_ref[rows(s), :])
        c_ref[s] = f[3]
        return f

    loop(forward, f)

    def backward(s, b):
        p, q = poles_of(d_ref[rows(s), :])
        b = cascade_source(p, q, b, c_ref[s])
        out_ref[rows(s), :] = b[3]
        return b

    loop(backward, b, reverse=True)


def x_first(arguments_ref, vt_ref, y_reach_ref, source_ref, d_ref, half_ref, chunks_ref, reach_ref, pair_ref):
    for z, here in enumerate(planes()):
        vt_ref[here, :] = arguments_ref[here, :].T
        spread(source_ref, z, arguments_ref[here, :])
    reach_ref[...] = arguments_ref[512:516, :]
    y_reach_ref[...] = arguments_ref[516:520, :]
    summarise(arguments_ref, source_ref, reach_ref, d_ref, half_ref, chunks_ref, pair_ref)


def x_second_y_first(
    vt_ref, reach_ref, source_ref, dx_ref, xhalf_ref, state_ref,
    t_ref, d_ref, half_ref, chunks_ref,
    ends_ref, c_ref, across_ref, wide_ref, pair_ref,
):
    ends_ref[...] = dx_ref[...]
    finish(source_ref, xhalf_ref, state_ref, ends_ref, c_ref, across_ref, wide_ref)
    for z in range(4):
        spread(t_ref, z, gather(across_ref, z).T)
    summarise(vt_ref, t_ref, reach_ref, d_ref, half_ref, chunks_ref, pair_ref)


def y_second(t_ref, d_ref, half_ref, state_ref, out_ref, ends_ref, c_ref, done_ref, wide_ref):
    ends_ref[...] = d_ref[...]
    finish(t_ref, half_ref, state_ref, ends_ref, c_ref, done_ref, wide_ref)
    for z, here in enumerate(planes()):
        out_ref[here, :] = gather(done_ref, z).T


def with_ends(block, first, last, source_first, source_last):
    A, u, B, C, w = block
    one, zero = jnp.ones_like(first), jnp.zeros_like(first)
    identity = {(k, j): one if k == j else zero for k, j in LOWER}
    p, q = poles_of(last)
    A, u = cascade_lower(p, q, A), cascade_source(p, q, u, source_last)
    inner = lower_times(B, cascade_source(p, q, [zero] * 4, one))
    B = lower_product(B, cascade_lower(p, q, identity))
    C = {(k, j): C[k, j] + inner[k] * A[3, j] for k, j in FULL}
    w = [x + y * u[3] for x, y in zip(w, inner)]
    p, q = poles_of(first)
    T, t = cascade_lower(p, q, identity), cascade_source(p, q, [zero] * 4, source_first)
    w = plus(w, full_times(C, t))
    u = plus(u, lower_times(A, t))
    A = lower_product(A, T)
    C = {(k, j): total([C[k, i] * T[i, j] for i in range(j, 4)]) for k, j in FULL}
    columns = [cascade_source(p, q, [C[k, j] for k in range(4)], T[3, j]) for j in range(4)]
    C = {(k, j): columns[j][k] for k, j in FULL}
    w = cascade_source(p, q, w, t[3])
    B = cascade_lower(p, q, B)
    return A, u, B, C, w


def line_scan(groups, blocks_ref, state_ref, map_ref, f_ref, b_ref):
    count, width = blocks_ref.shape[0], 128 // groups
    eights = count // 8
    row = lax.broadcasted_iota(jnp.int32, (8, 128), 0)
    group = lax.broadcasted_iota(jnp.int32, (8, 128), 1) // width

    def moved(x, by):
        by = by * width % 128
        return pltpu.roll(x, by, 1) if by else x

    def value(n):
        parts = [moved(blocks_ref[8 * g : 8 * g + 8, n // groups // 2, n // groups % 2, :], g - n % groups) for g in range(eights)]
        x = parts[0]
        for g in range(1, eights):
            x = jnp.where(group == g, parts[g], x)
        return x

    v = [value(37 + n) for n in range(4)]
    below = pltpu.roll(v[3], 1, 0)
    below = jnp.where(row == 0, jnp.where(group == 0, 0.0, moved(below, 1)), below)
    above = pltpu.roll(v[0], 7, 0)
    above = jnp.where(row == 7, jnp.where(group == eights - 1, 0.0, moved(above, -1)), above)
    inverse = -1.0 / value(43)
    first, last = (
        jnp.exp((1.0 + edge_slope * jnp.abs(gradient)) * inverse) for gradient in (0.5 * (v[1] - below), 0.5 * (above - v[2]))
    )
    block = with_ends(unpack(value), first, last, value(41), value(42))
    for n, x in enumerate(pack(block)):
        map_ref[n] = x

    def block_at(m):
        return unpack(lambda n: map_ref[n, m : m + 1, :])

    for reach in (1, 2, 4):
        other = tuple(
            {key: pltpu.roll(x, 8 - reach, 0) for key, x in part.items()} if isinstance(part, dict) else [pltpu.roll(x, 8 - reach, 0) for x in part]
            for part in block
        )
        block = compose(block, other)
    joined = unpack(lambda n, values=pack(block): values[n][0:1])

    here = group[0:1]
    zero = [jnp.zeros((1, 128), jnp.float32)] * 4
    f = zero
    for g in range(1, eights):
        through = [moved(x, 1) for x in forward_out(joined, f)]
        f = [jnp.where(here == g, x, y) for x, y in zip(through, f)]
    b = zero
    for g in reversed(range(eights - 1)):
        through = [moved(x, -1) for x in backward_out(joined, f, b)]
        b = [jnp.where(here == g, x, y) for x, y in zip(through, b)]

    inside = []
    for m in range(8):
        for k in range(4):
            f_ref[k, m : m + 1, :] = f[k]
        inside.append(f)
        f = forward_out(block_at(m), f)
    for m in reversed(range(8)):
        for k in range(4):
            b_ref[k, m : m + 1, :] = b[k]
        b = backward_out(block_at(m), inside[m], b)

    back = [f_ref[k] for k in range(4)] + [b_ref[k] for k in range(4)] + [first, last]
    for g in range(eights):
        some = slice(8 * g, 8 * g + 8)
        for start in range(0, 10, groups):
            x = moved(back[start], -g)
            for n in range(1, min(groups, 10 - start)):
                x = jnp.where(group == n, moved(back[start + n], n - g), x)
            state_ref[some, start // groups, :] = x
    for r in range(-(-10 // groups), state_ref.shape[1]):
        state_ref[:, r, :] = jnp.zeros((count, 128), jnp.float32)


def plane_scan(here_ref, blocks_ref, state_ref, map_ref, f_ref, b_ref):
    count = blocks_ref.shape[0]
    row = lax.broadcasted_iota(jnp.int32, (count, 128), 0)
    value = lambda n, some=slice(None): blocks_ref[some, n // 4, n % 4, :]
    v = [value(37 + n) for n in range(4)]
    below = jnp.where(row == 0, 0.0, pltpu.roll(v[3], 1, 0))
    above = jnp.where(row == count - 1, 0.0, pltpu.roll(v[0], count - 1, 0))
    inverse = -1.0 / value(43)
    for n, gradient in enumerate((0.5 * (v[1] - below), 0.5 * (above - v[2]))):
        map_ref[37 + n] = jnp.exp((1.0 + edge_slope * jnp.abs(gradient)) * inverse)
    for start in range(0, count, 8):
        some = slice(start, start + 8)
        block = unpack(lambda n: value(n, some))
        block = with_ends(block, map_ref[37, some, :], map_ref[38, some, :], value(41, some), value(42, some))
        for n, x in enumerate(pack(block)):
            map_ref[n, some, :] = x

    def block_at(m):
        return unpack(lambda n: map_ref[n, m : m + 1, :])

    f = [jnp.zeros((1, 128), jnp.float32)] * 4
    for m in range(count):
        for k in range(4):
            f_ref[k, m : m + 1, :] = f[k]
        f = forward_out(block_at(m), f)
    b = [jnp.zeros((1, 128), jnp.float32)] * 4
    for m in reversed(range(count)):
        for k in range(4):
            b_ref[k, m : m + 1, :] = b[k]
        b = backward_out(block_at(m), [f_ref[k, m : m + 1, :] for k in range(4)], b)

    here = here_ref[...]

    def mine(at):
        x = at(0)
        for g in range(1, count // 4):
            x = jnp.where(here == g, at(g), x)
        return x

    for k in range(4):
        state_ref[:, k, :] = mine(lambda g: f_ref[k, 4 * g : 4 * g + 4, :])
        state_ref[:, 4 + k, :] = mine(lambda g: b_ref[k, 4 * g : 4 * g + 4, :])
    for n in range(2):
        state_ref[:, 8 + n, :] = mine(lambda g: map_ref[37 + n, 4 * g : 4 * g + 4, :])
    for n in range(10, 16):
        state_ref[:, n, :] = jnp.zeros((4, 128), jnp.float32)


f32 = lambda *shape: jax.ShapeDtypeStruct(shape, jnp.float32)
vmem = lambda *shape: pltpu.VMEM(shape, jnp.float32)
plane = (512, 128)


def call(kernel, out_shape, scratch, *operands):
    return pl.pallas_call(kernel, out_shape=out_shape, scratch_shapes=scratch, compiler_params=params)(*operands)


def states(chunks, axis):
    size = lax.axis_size(axis)
    groups = size // 4
    chunks = lax.all_to_all(chunks, axis, 0, 0, tiled=True)
    scratch = [vmem(37, 8, 128), vmem(4, 8, 128), vmem(4, 8, 128)]
    entering = call(functools.partial(line_scan, groups), f32(size, 16 // groups, 128), scratch, chunks)
    return lax.all_to_all(entering, axis, 0, 0, tiled=True)


def states_by_planes(chunks, axis, group):
    size = lax.axis_size(axis)
    blocks = lax.all_to_all(chunks, axis, 0, 0, tiled=True)
    entering = call(plane_scan, f32(4, 16, 128), [vmem(39, size, 128), vmem(4, size, 128), vmem(4, size, 128)], group, blocks)
    fours = [[4 * g + i for i in range(4)] for g in range(size // 4)]
    return lax.all_to_all(entering, axis, 0, 0, axis_index_groups=fours, tiled=True)


def per_device(intensity, reach_along_x, reach_along_y):
    def maps(axis):
        size = lax.axis_size(axis)
        return [f32(*padded), f32(37, 8, 128), f32(size, 11, 4, 128) if axis == "gy" else f32(size, SLOTS * 2 // size, 2, 128)]

    group = jnp.full((4, 128), lax.shift_right_logical(lax.axis_index("gy"), 2), jnp.int32)

    work = [vmem(SLOTS * APART, 128)]
    ending = [vmem(*padded), vmem(STEPS, 8, 128), vmem(*padded), vmem(8 * APART, 128)]
    vt, y_reach, source, dx, x_half, x_chunks = call(
        x_first, [f32(*plane), f32(4, 128), f32(*padded)] + maps("gx"), [vmem(4, 128)] + work,
        jnp.concatenate([intensity.reshape(plane), reach_along_x, reach_along_y]),
    )
    x_states = states(x_chunks, "gx")
    t, dy, y_half, y_chunks = call(
        x_second_y_first, [f32(*padded)] + maps("gy"), ending + work, vt, y_reach, source, dx, x_half, x_states
    )
    y_states = states_by_planes(y_chunks, "gy", group)
    out = call(y_second, f32(*plane), ending, t, dy, y_half, y_states)
    return out.reshape(4, 128, 128)


def solution(mesh):
    return jax.shard_map(
        per_device,
        mesh=mesh,
        in_specs=(P(None, "gx", "gy"), P(None, "gy"), P(None, "gx")),
        out_specs=P(None, "gx", "gy"),
        check_vma=False,
    )
```

```python
import functools

import jax
import jax.numpy as jnp
from jax import lax
from jax.experimental import pallas as pl
from jax.experimental.pallas import tpu as pltpu
from jax.sharding import PartitionSpec as P

edge_slope = 3.0

LOWER = [(k, j) for k in range(4) for j in range(k + 1)]
BELOW = [(k, j) for k in range(4) for j in range(k)]
FULL = [(k, j) for k in range(4) for j in range(4)]
VALUES = 37

params = pltpu.CompilerParams(vmem_limit_bytes=48 * 1024 * 1024)
MATRICES = 29
SLOTS = 48
APART = 9


def unpack_matrices(get):
    A, B = {}, {}
    for n, kj in enumerate(BELOW):
        A[kj], B[kj] = get(1 + n), get(7 + n)
    power = get(0)
    for k in range(4):
        A[k, k] = B[k, k] = power
        power = power * power
    return A, B, {kj: get(13 + n) for n, kj in enumerate(FULL)}


def pack_matrices(matrices):
    A, B, C = matrices
    return [A[0, 0]] + [A[kj] for kj in BELOW] + [B[kj] for kj in BELOW] + [C[kj] for kj in FULL]


def unpack(get):
    A, B, C = unpack_matrices(get)
    vectors = [get(MATRICES + n) for n in range(8)]
    return A, vectors[:4], B, C, vectors[4:]


def pack(block):
    A, u, B, C, w = block
    return pack_matrices((A, B, C)) + list(u) + list(w)


def total(terms):
    terms = list(terms)
    while len(terms) > 1:
        terms = [a + b for a, b in zip(terms[::2], terms[1::2])] + terms[len(terms) - len(terms) % 2 :]
    return terms[0]


def lower_times(M, x):
    return [total([M[k, j] * x[j] for j in range(k + 1)]) for k in range(4)]


def full_times(M, x):
    return [total([M[k, j] * x[j] for j in range(4)]) for k in range(4)]


def plus(x, y):
    return [a + b for a, b in zip(x, y)]


def lower_product(M, N):
    return {(k, j): total([M[k, i] * N[i, j] for i in range(j, k + 1)]) for k, j in LOWER}


def compose_matrices(left, right):
    A1, B1, C1 = left
    A2, B2, C2 = right
    A = lower_product(A2, A1)
    B = lower_product(B1, B2)
    CA = {(k, j): total([C2[k, i] * A1[i, j] for i in range(j, 4)]) for k, j in FULL}
    C = {(k, j): total([B1[k, i] * CA[i, j] for i in range(k + 1)]) + C1[k, j] for k, j in FULL}
    return A, B, C


def compose_vectors(B1, A2, C2, left, right):
    u1, w1 = left
    u2, w2 = right
    u = plus(lower_times(A2, u1), u2)
    w = plus(lower_times(B1, plus(full_times(C2, u1), w2)), w1)
    return u, w


def compose(left, right):
    A1, u1, B1, C1, w1 = left
    A2, u2, B2, C2, w2 = right
    A, B, C = compose_matrices((A1, B1, C1), (A2, B2, C2))
    u, w = compose_vectors(B1, A2, C2, (u1, w1), (u2, w2))
    return A, u, B, C, w


def forward_out(block, f):
    A, u = block[:2]
    return [total([A[k, j] * f[j] for j in range(k + 1)] + [u[k]]) for k in range(4)]


def backward_out(block, f, b):
    B, C, w = block[2:]
    return [total([B[k, j] * b[j] for j in range(k + 1)] + [C[k, j] * f[j] for j in range(4)] + [w[k]]) for k in range(4)]


def poles_of(d):
    p = [d]
    for _ in range(3):
        p.append(p[-1] * p[-1])
    return p, [1.0 - x for x in p]


STEPS, UNROLL = 64, 16
PITCH = 65
padded = (8 * PITCH, 128)


def loop(body, carry, reverse=False):
    def some(n, carry):
        for k in range(UNROLL):
            at = n * UNROLL + k
            carry = body(STEPS - 1 - at if reverse else at, carry)
        return carry

    return lax.fori_loop(0, STEPS // UNROLL, some, carry)


def rows(s):
    return pl.ds(s, 8, stride=PITCH)


def decay_block(v, inverse):
    at = lax.broadcasted_iota(jnp.int32, v.shape, 0)
    n = v.shape[0]
    gradient = 0.5 * (pltpu.roll(v, n - 1, 0) - pltpu.roll(v, 1, 0))
    d = jnp.exp((1.0 + edge_slope * jnp.abs(gradient)) * inverse)
    return jnp.where((at == 0) | (at == n - 1), 1.0, d)


def cascade_lower(p, q, M):
    M = dict(M)
    for j in range(4):
        M[j, j] = p[j] * M[j, j]
        for k in range(j + 1, 4):
            M[k, j] = p[k] * M[k, j] + q[k] * M[k - 1, j]
    return M


def cascade_source(p, q, x, source):
    x = list(x)
    for k in range(4):
        x[k] = p[k] * x[k] + q[k] * (source if k == 0 else x[k - 1])
    return x


def before_step(p, q, B):
    new, inner = {}, []
    for k in range(4):
        carried = B[k, k]
        new[k, k] = p[k] * carried
        for j in reversed(range(k)):
            carried = B[k, j] + q[j + 1] * carried
            new[k, j] = p[j] * carried
        inner.append(q[0] * carried)
    return new, inner


def half_maps(v_ref, d_ref):
    one, zero = jnp.ones((8, 128), jnp.float32), jnp.zeros((8, 128), jnp.float32)

    def step(s, carry):
        A, u, B, C, w = carry
        A, B = dict(zip(LOWER, A)), dict(zip(LOWER, B))
        p, q = poles_of(d_ref[rows(s), :])
        u = cascade_source(p, q, u, v_ref[rows(s), :])
        A = cascade_lower(p, q, A)
        B, inner = before_step(p, q, B)
        C = [c + inner[k] * A[3, j] for c, (k, j) in zip(C, FULL)]
        w = [x + y * u[3] for x, y in zip(w, inner)]
        return [A[kj] for kj in LOWER], u, [B[kj] for kj in LOWER], C, w

    start = [one if k == j else zero for k, j in LOWER]
    A, u, B, C, w = loop(step, (start, [zero] * 4, start, [zero] * 16, [zero] * 4))
    return dict(zip(LOWER, A)), u, dict(zip(LOWER, B)), dict(zip(FULL, C)), w


def after(part):
    if isinstance(part, dict):
        return {key: pltpu.roll(x, 7, 0) for key, x in part.items()}
    return [pltpu.roll(x, 7, 0) for x in part]


def planes():
    return [slice(z * 128, (z + 1) * 128) for z in range(4)]


def place(i):
    return pl.ds(i // STEPS * PITCH + i % STEPS, 4, stride=2 * PITCH)


def spread(ref, z, block):
    for h in range(2):
        at = (2 * z + h) * PITCH
        ref[at : at + STEPS, :] = block[h * STEPS : (h + 1) * STEPS]


def gather(ref, z):
    at = 2 * z * PITCH
    return jnp.concatenate([ref[at : at + STEPS, :], ref[at + PITCH : at + PITCH + STEPS, :]], axis=0)


def swap(x, groups):
    row, lane = (lax.broadcasted_iota(jnp.int32, x.shape, axis) for axis in range(2))
    width = 128 // groups
    t = 1
    while t < groups:
        lower, right = (row // t) % 2 == 1, (lane // (width * t)) % 2 == 1
        up = pltpu.roll(pltpu.roll(x, 8 - t, 0), width * t, 1)
        down = pltpu.roll(pltpu.roll(x, t, 0), 128 - width * t, 1)
        x = jnp.where(lower == right, x, jnp.where(lower, down, up))
        t *= 2
    return x


def summarise(v_ref, source_ref, reach_ref, d_ref, half_ref, chunks_ref, pair_ref):
    for z, here in enumerate(planes()):
        spread(d_ref, z, decay_block(v_ref[here, :], -1.0 / reach_ref[z : z + 1, :]))
    block = half_maps(source_ref, d_ref)
    for n, value in enumerate(pack(block)):
        half_ref[n] = value
    for n, value in enumerate(pack(compose(block, tuple(after(part) for part in block)))):
        pair_ref[n * APART : n * APART + 8, :] = value
    ends = [v_ref[pl.ds(i, 4, stride=128), :] for i in (0, 1, 126, 127)] + [source_ref[place(0), :], source_ref[place(127), :], reach_ref[...]]
    for n, value in enumerate(ends):
        pair_ref[pl.ds((37 + n) * APART, 4, stride=2), :] = value
    for n in range(44, SLOTS):
        pair_ref[n * APART : n * APART + 8, :] = jnp.zeros((8, 128), jnp.float32)
    if chunks_ref.shape[2] == 4:
        for z in range(4):
            for n in range(0, 44, 4):
                x = pair_ref[pl.ds(n * APART + 2 * z, 4, stride=APART), :]
                for at in range(z, chunks_ref.shape[0], 4):
                    chunks_ref[at, n // 4] = x
        return
    per_plane = chunks_ref.shape[0] // 4
    groups = per_plane
    for z in range(4):
        chunks = slice(z * per_plane, (z + 1) * per_plane)
        for n in range(0, SLOTS, 8):
            x = swap(pair_ref[pl.ds(n * APART + 2 * z, 8, stride=APART), :], groups)
            for a in range(8 // groups):
                r = n // groups + a
                chunks_ref[chunks, r // 2, r % 2, :] = x[a * groups : (a + 1) * groups]


def finish(v_ref, half_ref, state_ref, d_ref, c_ref, out_ref, wide_ref):
    groups = state_ref.shape[0] // 4
    for z in range(4):
        chunks = slice(z * groups, (z + 1) * groups)
        if groups == 1:
            x, ends = state_ref[z, 0:8, :], state_ref[z, 8:16, :]
        else:
            count = 8 // groups
            x = swap(jnp.concatenate([state_ref[chunks, a, :] for a in range(count)], axis=0), groups)
            ends = swap(jnp.concatenate([state_ref[chunks, count, :]] * count, axis=0), groups)
        wide_ref[pl.ds(2 * z, 8, stride=APART), :] = x
        wide_ref[pl.ds(2 * z + 1, 8, stride=APART), :] = x
        first, last = 2 * z * PITCH, (2 * z + 1) * PITCH + STEPS - 1
        d_ref[first : first + 1, :] = ends[0:1]
        d_ref[last : last + 1, :] = ends[1:2]
    f = [wide_ref[k * APART : k * APART + 8, :] for k in range(4)]
    b = [wide_ref[k * APART : k * APART + 8, :] for k in range(4, 8)]
    block = unpack(lambda n: half_ref[n])
    second = lax.broadcasted_iota(jnp.int32, (8, 128), 0) % 2 == 1
    p, q = poles_of(d_ref[rows(0), :])
    f_middle = [pltpu.roll(x, 1, 0) for x in forward_out(block, cascade_source(p, q, f, v_ref[rows(0), :]))]
    p, q = poles_of(d_ref[rows(STEPS - 1), :])
    f_last = cascade_source(p, q, forward_out(block, f_middle), v_ref[rows(STEPS - 1), :])
    b_middle = [pltpu.roll(x, 7, 0) for x in backward_out(block, f_middle, cascade_source(p, q, b, f_last[3]))]
    f = [jnp.where(second, x, y) for x, y in zip(f_middle, f)]
    b = [jnp.where(second, y, x) for x, y in zip(b_middle, b)]

    def forward(s, f):
        p, q = poles_of(d_ref[rows(s), :])
        f = cascade_source(p, q, f, v_ref[rows(s), :])
        c_ref[s] = f[3]
        return f

    loop(forward, f)

    def backward(s, b):
        p, q = poles_of(d_ref[rows(s), :])
        b = cascade_source(p, q, b, c_ref[s])
        out_ref[rows(s), :] = b[3]
        return b

    loop(backward, b, reverse=True)


def x_first(arguments_ref, here_ref, vt_ref, y_reach_ref, group_ref, source_ref, d_ref, half_ref, chunks_ref, reach_ref, pair_ref):
    for z, here in enumerate(planes()):
        vt_ref[here, :] = arguments_ref[here, :].T
        spread(source_ref, z, arguments_ref[here, :])
    group_ref[...] = here_ref[...]
    reach_ref[...] = arguments_ref[512:516, :]
    y_reach_ref[...] = arguments_ref[516:520, :]
    summarise(arguments_ref, source_ref, reach_ref, d_ref, half_ref, chunks_ref, pair_ref)


def x_second_y_first(
    vt_ref, reach_ref, source_ref, dx_ref, xhalf_ref, state_ref,
    t_ref, d_ref, half_ref, chunks_ref,
    ends_ref, c_ref, across_ref, wide_ref, pair_ref,
):
    ends_ref[...] = dx_ref[...]
    finish(source_ref, xhalf_ref, state_ref, ends_ref, c_ref, across_ref, wide_ref)
    for z in range(4):
        spread(t_ref, z, gather(across_ref, z).T)
    summarise(vt_ref, t_ref, reach_ref, d_ref, half_ref, chunks_ref, pair_ref)


def y_second(t_ref, d_ref, half_ref, state_ref, out_ref, ends_ref, c_ref, done_ref, wide_ref):
    ends_ref[...] = d_ref[...]
    finish(t_ref, half_ref, state_ref, ends_ref, c_ref, done_ref, wide_ref)
    for z, here in enumerate(planes()):
        out_ref[here, :] = gather(done_ref, z).T


def with_ends(block, first, last, source_first, source_last):
    A, u, B, C, w = block
    one, zero = jnp.ones_like(first), jnp.zeros_like(first)
    identity = {(k, j): one if k == j else zero for k, j in LOWER}
    p, q = poles_of(last)
    A, u = cascade_lower(p, q, A), cascade_source(p, q, u, source_last)
    inner = lower_times(B, cascade_source(p, q, [zero] * 4, one))
    B = lower_product(B, cascade_lower(p, q, identity))
    C = {(k, j): C[k, j] + inner[k] * A[3, j] for k, j in FULL}
    w = [x + y * u[3] for x, y in zip(w, inner)]
    p, q = poles_of(first)
    T, t = cascade_lower(p, q, identity), cascade_source(p, q, [zero] * 4, source_first)
    w = plus(w, full_times(C, t))
    u = plus(u, lower_times(A, t))
    A = lower_product(A, T)
    C = {(k, j): total([C[k, i] * T[i, j] for i in range(j, 4)]) for k, j in FULL}
    columns = [cascade_source(p, q, [C[k, j] for k in range(4)], T[3, j]) for j in range(4)]
    C = {(k, j): columns[j][k] for k, j in FULL}
    w = cascade_source(p, q, w, t[3])
    B = cascade_lower(p, q, B)
    return A, u, B, C, w


def line_scan(groups, blocks_ref, state_ref, map_ref, f_ref, b_ref):
    count, width = blocks_ref.shape[0], 128 // groups
    eights = count // 8
    row = lax.broadcasted_iota(jnp.int32, (8, 128), 0)
    group = lax.broadcasted_iota(jnp.int32, (8, 128), 1) // width

    def moved(x, by):
        by = by * width % 128
        return pltpu.roll(x, by, 1) if by else x

    def value(n):
        parts = [moved(blocks_ref[8 * g : 8 * g + 8, n // groups // 2, n // groups % 2, :], g - n % groups) for g in range(eights)]
        x = parts[0]
        for g in range(1, eights):
            x = jnp.where(group == g, parts[g], x)
        return x

    v = [value(37 + n) for n in range(4)]
    below = pltpu.roll(v[3], 1, 0)
    below = jnp.where(row == 0, jnp.where(group == 0, 0.0, moved(below, 1)), below)
    above = pltpu.roll(v[0], 7, 0)
    above = jnp.where(row == 7, jnp.where(group == eights - 1, 0.0, moved(above, -1)), above)
    inverse = -1.0 / value(43)
    first, last = (
        jnp.exp((1.0 + edge_slope * jnp.abs(gradient)) * inverse) for gradient in (0.5 * (v[1] - below), 0.5 * (above - v[2]))
    )
    block = with_ends(unpack(value), first, last, value(41), value(42))
    for n, x in enumerate(pack(block)):
        map_ref[n] = x

    def block_at(m):
        return unpack(lambda n: map_ref[n, m : m + 1, :])

    for reach in (1, 2, 4):
        other = tuple(
            {key: pltpu.roll(x, 8 - reach, 0) for key, x in part.items()} if isinstance(part, dict) else [pltpu.roll(x, 8 - reach, 0) for x in part]
            for part in block
        )
        block = compose(block, other)
    joined = unpack(lambda n, values=pack(block): values[n][0:1])

    here = group[0:1]
    zero = [jnp.zeros((1, 128), jnp.float32)] * 4
    f = zero
    for g in range(1, eights):
        through = [moved(x, 1) for x in forward_out(joined, f)]
        f = [jnp.where(here == g, x, y) for x, y in zip(through, f)]
    b = zero
    for g in reversed(range(eights - 1)):
        through = [moved(x, -1) for x in backward_out(joined, f, b)]
        b = [jnp.where(here == g, x, y) for x, y in zip(through, b)]

    inside = []
    for m in range(8):
        for k in range(4):
            f_ref[k, m : m + 1, :] = f[k]
        inside.append(f)
        f = forward_out(block_at(m), f)
    for m in reversed(range(8)):
        for k in range(4):
            b_ref[k, m : m + 1, :] = b[k]
        b = backward_out(block_at(m), inside[m], b)

    back = [f_ref[k] for k in range(4)] + [b_ref[k] for k in range(4)] + [first, last]
    for g in range(eights):
        some = slice(8 * g, 8 * g + 8)
        for start in range(0, 10, groups):
            x = moved(back[start], -g)
            for n in range(1, min(groups, 10 - start)):
                x = jnp.where(group == n, moved(back[start + n], n - g), x)
            state_ref[some, start // groups, :] = x
    for r in range(-(-10 // groups), state_ref.shape[1]):
        state_ref[:, r, :] = jnp.zeros((count, 128), jnp.float32)


def plane_scan(here_ref, blocks_ref, state_ref, map_ref, f_ref, b_ref):
    count = blocks_ref.shape[0]
    row = lax.broadcasted_iota(jnp.int32, (count, 128), 0)
    value = lambda n, some=slice(None): blocks_ref[some, n // 4, n % 4, :]
    v = [value(37 + n) for n in range(4)]
    below = jnp.where(row == 0, 0.0, pltpu.roll(v[3], 1, 0))
    above = jnp.where(row == count - 1, 0.0, pltpu.roll(v[0], count - 1, 0))
    inverse = -1.0 / value(43)
    for n, gradient in enumerate((0.5 * (v[1] - below), 0.5 * (above - v[2]))):
        map_ref[37 + n] = jnp.exp((1.0 + edge_slope * jnp.abs(gradient)) * inverse)
    for start in range(0, count, 8):
        some = slice(start, start + 8)
        block = unpack(lambda n: value(n, some))
        block = with_ends(block, map_ref[37, some, :], map_ref[38, some, :], value(41, some), value(42, some))
        for n, x in enumerate(pack(block)):
            map_ref[n, some, :] = x

    def block_at(m):
        return unpack(lambda n: map_ref[n, m : m + 1, :])

    f = [jnp.zeros((1, 128), jnp.float32)] * 4
    for m in range(count):
        for k in range(4):
            f_ref[k, m : m + 1, :] = f[k]
        f = forward_out(block_at(m), f)
    b = [jnp.zeros((1, 128), jnp.float32)] * 4
    for m in reversed(range(count)):
        for k in range(4):
            b_ref[k, m : m + 1, :] = b[k]
        b = backward_out(block_at(m), [f_ref[k, m : m + 1, :] for k in range(4)], b)

    here = here_ref[...]

    def mine(at):
        x = at(0)
        for g in range(1, count // 4):
            x = jnp.where(here == g, at(g), x)
        return x

    for k in range(4):
        state_ref[:, k, :] = mine(lambda g: f_ref[k, 4 * g : 4 * g + 4, :])
        state_ref[:, 4 + k, :] = mine(lambda g: b_ref[k, 4 * g : 4 * g + 4, :])
    for n in range(2):
        state_ref[:, 8 + n, :] = mine(lambda g: map_ref[37 + n, 4 * g : 4 * g + 4, :])
    for n in range(10, 16):
        state_ref[:, n, :] = jnp.zeros((4, 128), jnp.float32)


f32 = lambda *shape: jax.ShapeDtypeStruct(shape, jnp.float32)
vmem = lambda *shape: pltpu.VMEM(shape, jnp.float32)
plane = (512, 128)


def call(kernel, out_shape, scratch, *operands):
    return pl.pallas_call(kernel, out_shape=out_shape, scratch_shapes=scratch, compiler_params=params)(*operands)


def states(chunks, axis):
    size = lax.axis_size(axis)
    groups = size // 4
    chunks = lax.all_to_all(chunks, axis, 0, 0, tiled=True)
    scratch = [vmem(37, 8, 128), vmem(4, 8, 128), vmem(4, 8, 128)]
    entering = call(functools.partial(line_scan, groups), f32(size, 16 // groups, 128), scratch, chunks)
    return lax.all_to_all(entering, axis, 0, 0, tiled=True)


def states_by_planes(chunks, axis, group):
    size = lax.axis_size(axis)
    blocks = lax.all_to_all(chunks, axis, 0, 0, tiled=True)
    entering = call(plane_scan, f32(4, 16, 128), [vmem(39, size, 128), vmem(4, size, 128), vmem(4, size, 128)], group, blocks)
    fours = [[4 * g + i for i in range(4)] for g in range(size // 4)]
    return lax.all_to_all(entering, axis, 0, 0, axis_index_groups=fours, tiled=True)


def per_device(intensity, reach_along_x, reach_along_y):
    def maps(axis):
        size = lax.axis_size(axis)
        return [f32(*padded), f32(37, 8, 128), f32(size, 11, 4, 128) if axis == "gy" else f32(size, SLOTS * 2 // size, 2, 128)]

    group = jnp.full((4, 128), lax.shift_right_logical(lax.axis_index("gy"), 2), jnp.int32)

    work = [vmem(SLOTS * APART, 128)]
    ending = [vmem(*padded), vmem(STEPS, 8, 128), vmem(*padded), vmem(8 * APART, 128)]
    vt, y_reach, group, source, dx, x_half, x_chunks = call(
        x_first, [f32(*plane), f32(4, 128), jax.ShapeDtypeStruct((4, 128), jnp.int32), f32(*padded)] + maps("gx"), [vmem(4, 128)] + work,
        jnp.concatenate([intensity.reshape(plane), reach_along_x, reach_along_y]), group,
    )
    x_states = states(x_chunks, "gx")
    t, dy, y_half, y_chunks = call(
        x_second_y_first, [f32(*padded)] + maps("gy"), ending + work, vt, y_reach, source, dx, x_half, x_states
    )
    y_states = states_by_planes(y_chunks, "gy", group)
    out = call(y_second, f32(*plane), ending, t, dy, y_half, y_states)
    return out.reshape(4, 128, 128)


def solution(mesh):
    return jax.shard_map(
        per_device,
        mesh=mesh,
        in_specs=(P(None, "gx", "gy"), P(None, "gy"), P(None, "gx")),
        out_specs=P(None, "gx", "gy"),
        check_vma=False,
    )
```

```python
import functools

import jax
import jax.numpy as jnp
from jax import lax
from jax.experimental import pallas as pl
from jax.experimental.pallas import tpu as pltpu
from jax.sharding import PartitionSpec as P

edge_slope = 3.0

LOWER = [(k, j) for k in range(4) for j in range(k + 1)]
BELOW = [(k, j) for k in range(4) for j in range(k)]
FULL = [(k, j) for k in range(4) for j in range(4)]
VALUES = 37

params = pltpu.CompilerParams(vmem_limit_bytes=48 * 1024 * 1024)
MATRICES = 29
SLOTS = 48
APART = 9


def unpack_matrices(get):
    A, B = {}, {}
    for n, kj in enumerate(BELOW):
        A[kj], B[kj] = get(1 + n), get(7 + n)
    power = get(0)
    for k in range(4):
        A[k, k] = B[k, k] = power
        power = power * power
    return A, B, {kj: get(13 + n) for n, kj in enumerate(FULL)}


def pack_matrices(matrices):
    A, B, C = matrices
    return [A[0, 0]] + [A[kj] for kj in BELOW] + [B[kj] for kj in BELOW] + [C[kj] for kj in FULL]


def unpack(get):
    A, B, C = unpack_matrices(get)
    vectors = [get(MATRICES + n) for n in range(8)]
    return A, vectors[:4], B, C, vectors[4:]


def pack(block):
    A, u, B, C, w = block
    return pack_matrices((A, B, C)) + list(u) + list(w)


def total(terms):
    terms = list(terms)
    while len(terms) > 1:
        terms = [a + b for a, b in zip(terms[::2], terms[1::2])] + terms[len(terms) - len(terms) % 2 :]
    return terms[0]


def lower_times(M, x):
    return [total([M[k, j] * x[j] for j in range(k + 1)]) for k in range(4)]


def full_times(M, x):
    return [total([M[k, j] * x[j] for j in range(4)]) for k in range(4)]


def plus(x, y):
    return [a + b for a, b in zip(x, y)]


def lower_product(M, N):
    return {(k, j): total([M[k, i] * N[i, j] for i in range(j, k + 1)]) for k, j in LOWER}


def compose_matrices(left, right):
    A1, B1, C1 = left
    A2, B2, C2 = right
    A = lower_product(A2, A1)
    B = lower_product(B1, B2)
    CA = {(k, j): total([C2[k, i] * A1[i, j] for i in range(j, 4)]) for k, j in FULL}
    C = {(k, j): total([B1[k, i] * CA[i, j] for i in range(k + 1)]) + C1[k, j] for k, j in FULL}
    return A, B, C


def compose_vectors(B1, A2, C2, left, right):
    u1, w1 = left
    u2, w2 = right
    u = plus(lower_times(A2, u1), u2)
    w = plus(lower_times(B1, plus(full_times(C2, u1), w2)), w1)
    return u, w


def compose(left, right):
    A1, u1, B1, C1, w1 = left
    A2, u2, B2, C2, w2 = right
    A, B, C = compose_matrices((A1, B1, C1), (A2, B2, C2))
    u, w = compose_vectors(B1, A2, C2, (u1, w1), (u2, w2))
    return A, u, B, C, w


def forward_out(block, f):
    A, u = block[:2]
    return [total([A[k, j] * f[j] for j in range(k + 1)] + [u[k]]) for k in range(4)]


def backward_out(block, f, b):
    B, C, w = block[2:]
    return [total([B[k, j] * b[j] for j in range(k + 1)] + [C[k, j] * f[j] for j in range(4)] + [w[k]]) for k in range(4)]


def poles_of(d):
    p = [d]
    for _ in range(3):
        p.append(p[-1] * p[-1])
    return p, [1.0 - x for x in p]


STEPS, UNROLL = 64, 16
PITCH = 65
padded = (8 * PITCH, 128)


def loop(body, carry, reverse=False):
    def some(n, carry):
        for k in range(UNROLL):
            at = n * UNROLL + k
            carry = body(STEPS - 1 - at if reverse else at, carry)
        return carry

    return lax.fori_loop(0, STEPS // UNROLL, some, carry)


def rows(s):
    return pl.ds(s, 8, stride=PITCH)


def decay_block(v, inverse):
    at = lax.broadcasted_iota(jnp.int32, v.shape, 0)
    n = v.shape[0]
    gradient = 0.5 * (pltpu.roll(v, n - 1, 0) - pltpu.roll(v, 1, 0))
    d = jnp.exp((1.0 + edge_slope * jnp.abs(gradient)) * inverse)
    return jnp.where((at == 0) | (at == n - 1), 1.0, d)


def cascade_lower(p, q, M):
    M = dict(M)
    for j in range(4):
        M[j, j] = p[j] * M[j, j]
        for k in range(j + 1, 4):
            M[k, j] = p[k] * M[k, j] + q[k] * M[k - 1, j]
    return M


def cascade_source(p, q, x, source):
    x = list(x)
    for k in range(4):
        x[k] = p[k] * x[k] + q[k] * (source if k == 0 else x[k - 1])
    return x


def before_step(p, q, B):
    new, inner = {}, []
    for k in range(4):
        carried = B[k, k]
        new[k, k] = p[k] * carried
        for j in reversed(range(k)):
            carried = B[k, j] + q[j + 1] * carried
            new[k, j] = p[j] * carried
        inner.append(q[0] * carried)
    return new, inner


def half_maps(v_ref, d_ref):
    one, zero = jnp.ones((8, 128), jnp.float32), jnp.zeros((8, 128), jnp.float32)

    def step(s, carry):
        A, u, B, C, w = carry
        A, B = dict(zip(LOWER, A)), dict(zip(LOWER, B))
        p, q = poles_of(d_ref[rows(s), :])
        u = cascade_source(p, q, u, v_ref[rows(s), :])
        A = cascade_lower(p, q, A)
        B, inner = before_step(p, q, B)
        C = [c + inner[k] * A[3, j] for c, (k, j) in zip(C, FULL)]
        w = [x + y * u[3] for x, y in zip(w, inner)]
        return [A[kj] for kj in LOWER], u, [B[kj] for kj in LOWER], C, w

    start = [one if k == j else zero for k, j in LOWER]
    A, u, B, C, w = loop(step, (start, [zero] * 4, start, [zero] * 16, [zero] * 4))
    return dict(zip(LOWER, A)), u, dict(zip(LOWER, B)), dict(zip(FULL, C)), w


def after(part):
    if isinstance(part, dict):
        return {key: pltpu.roll(x, 7, 0) for key, x in part.items()}
    return [pltpu.roll(x, 7, 0) for x in part]


def planes():
    return [slice(z * 128, (z + 1) * 128) for z in range(4)]


def place(i):
    return pl.ds(i // STEPS * PITCH + i % STEPS, 4, stride=2 * PITCH)


def spread(ref, z, block):
    for h in range(2):
        at = (2 * z + h) * PITCH
        ref[at : at + STEPS, :] = block[h * STEPS : (h + 1) * STEPS]


def gather(ref, z):
    at = 2 * z * PITCH
    return jnp.concatenate([ref[at : at + STEPS, :], ref[at + PITCH : at + PITCH + STEPS, :]], axis=0)


def swap(x, groups):
    row, lane = (lax.broadcasted_iota(jnp.int32, x.shape, axis) for axis in range(2))
    width = 128 // groups
    t = 1
    while t < groups:
        lower, right = (row // t) % 2 == 1, (lane // (width * t)) % 2 == 1
        up = pltpu.roll(pltpu.roll(x, 8 - t, 0), width * t, 1)
        down = pltpu.roll(pltpu.roll(x, t, 0), 128 - width * t, 1)
        x = jnp.where(lower == right, x, jnp.where(lower, down, up))
        t *= 2
    return x


def summarise(v_ref, source_ref, reach_ref, d_ref, half_ref, chunks_ref, pair_ref):
    for z, here in enumerate(planes()):
        spread(d_ref, z, decay_block(v_ref[here, :], -1.0 / reach_ref[z : z + 1, :]))
    block = half_maps(source_ref, d_ref)
    for n, value in enumerate(pack(block)):
        half_ref[n] = value
    for n, value in enumerate(pack(compose(block, tuple(after(part) for part in block)))):
        pair_ref[n * APART : n * APART + 8, :] = value
    ends = [v_ref[pl.ds(i, 4, stride=128), :] for i in (0, 1, 126, 127)] + [source_ref[place(0), :], source_ref[place(127), :], reach_ref[...]]
    for n, value in enumerate(ends):
        pair_ref[pl.ds((37 + n) * APART, 4, stride=2), :] = value
    for n in range(44, SLOTS):
        pair_ref[n * APART : n * APART + 8, :] = jnp.zeros((8, 128), jnp.float32)
    if chunks_ref.shape[2] == 4:
        row = lax.broadcasted_iota(jnp.int32, (4, 128), 0)
        for z in range(4):
            for n in range(0, 44, 4):
                x = pair_ref[pl.ds(n * APART + 2 * z, 4, stride=APART), :]
                for at in range(z, chunks_ref.shape[0], 4):
                    chunks_ref[at, n // 4] = x if n != 40 else jnp.where(row == 3, float(at), x)
        return
    per_plane = chunks_ref.shape[0] // 4
    groups = per_plane
    for z in range(4):
        chunks = slice(z * per_plane, (z + 1) * per_plane)
        for n in range(0, SLOTS, 8):
            x = swap(pair_ref[pl.ds(n * APART + 2 * z, 8, stride=APART), :], groups)
            for a in range(8 // groups):
                r = n // groups + a
                chunks_ref[chunks, r // 2, r % 2, :] = x[a * groups : (a + 1) * groups]


def finish(v_ref, half_ref, state_ref, d_ref, c_ref, out_ref, wide_ref):
    groups = state_ref.shape[0] // 4
    for z in range(4):
        chunks = slice(z * groups, (z + 1) * groups)
        if groups == 1:
            x, ends = state_ref[z, 0:8, :], state_ref[z, 8:16, :]
        else:
            count = 8 // groups
            x = swap(jnp.concatenate([state_ref[chunks, a, :] for a in range(count)], axis=0), groups)
            ends = swap(jnp.concatenate([state_ref[chunks, count, :]] * count, axis=0), groups)
        wide_ref[pl.ds(2 * z, 8, stride=APART), :] = x
        wide_ref[pl.ds(2 * z + 1, 8, stride=APART), :] = x
        first, last = 2 * z * PITCH, (2 * z + 1) * PITCH + STEPS - 1
        d_ref[first : first + 1, :] = ends[0:1]
        d_ref[last : last + 1, :] = ends[1:2]
    f = [wide_ref[k * APART : k * APART + 8, :] for k in range(4)]
    b = [wide_ref[k * APART : k * APART + 8, :] for k in range(4, 8)]
    block = unpack(lambda n: half_ref[n])
    second = lax.broadcasted_iota(jnp.int32, (8, 128), 0) % 2 == 1
    p, q = poles_of(d_ref[rows(0), :])
    f_middle = [pltpu.roll(x, 1, 0) for x in forward_out(block, cascade_source(p, q, f, v_ref[rows(0), :]))]
    p, q = poles_of(d_ref[rows(STEPS - 1), :])
    f_last = cascade_source(p, q, forward_out(block, f_middle), v_ref[rows(STEPS - 1), :])
    b_middle = [pltpu.roll(x, 7, 0) for x in backward_out(block, f_middle, cascade_source(p, q, b, f_last[3]))]
    f = [jnp.where(second, x, y) for x, y in zip(f_middle, f)]
    b = [jnp.where(second, y, x) for x, y in zip(b_middle, b)]

    def forward(s, f):
        p, q = poles_of(d_ref[rows(s), :])
        f = cascade_source(p, q, f, v_ref[rows(s), :])
        c_ref[s] = f[3]
        return f

    loop(forward, f)

    def backward(s, b):
        p, q = poles_of(d_ref[rows(s), :])
        b = cascade_source(p, q, b, c_ref[s])
        out_ref[rows(s), :] = b[3]
        return b

    loop(backward, b, reverse=True)


def x_first(arguments_ref, vt_ref, y_reach_ref, source_ref, d_ref, half_ref, chunks_ref, reach_ref, pair_ref):
    for z, here in enumerate(planes()):
        vt_ref[here, :] = arguments_ref[here, :].T
        spread(source_ref, z, arguments_ref[here, :])
    reach_ref[...] = arguments_ref[512:516, :]
    y_reach_ref[...] = arguments_ref[516:520, :]
    summarise(arguments_ref, source_ref, reach_ref, d_ref, half_ref, chunks_ref, pair_ref)


def x_second_y_first(
    vt_ref, reach_ref, source_ref, dx_ref, xhalf_ref, state_ref,
    t_ref, d_ref, half_ref, chunks_ref,
    ends_ref, c_ref, across_ref, wide_ref, pair_ref,
):
    ends_ref[...] = dx_ref[...]
    finish(source_ref, xhalf_ref, state_ref, ends_ref, c_ref, across_ref, wide_ref)
    for z in range(4):
        spread(t_ref, z, gather(across_ref, z).T)
    summarise(vt_ref, t_ref, reach_ref, d_ref, half_ref, chunks_ref, pair_ref)


def y_second(t_ref, d_ref, half_ref, state_ref, out_ref, ends_ref, c_ref, done_ref, wide_ref):
    ends_ref[...] = d_ref[...]
    finish(t_ref, half_ref, state_ref, ends_ref, c_ref, done_ref, wide_ref)
    for z, here in enumerate(planes()):
        out_ref[here, :] = gather(done_ref, z).T


def with_ends(block, first, last, source_first, source_last):
    A, u, B, C, w = block
    one, zero = jnp.ones_like(first), jnp.zeros_like(first)
    identity = {(k, j): one if k == j else zero for k, j in LOWER}
    p, q = poles_of(last)
    A, u = cascade_lower(p, q, A), cascade_source(p, q, u, source_last)
    inner = lower_times(B, cascade_source(p, q, [zero] * 4, one))
    B = lower_product(B, cascade_lower(p, q, identity))
    C = {(k, j): C[k, j] + inner[k] * A[3, j] for k, j in FULL}
    w = [x + y * u[3] for x, y in zip(w, inner)]
    p, q = poles_of(first)
    T, t = cascade_lower(p, q, identity), cascade_source(p, q, [zero] * 4, source_first)
    w = plus(w, full_times(C, t))
    u = plus(u, lower_times(A, t))
    A = lower_product(A, T)
    C = {(k, j): total([C[k, i] * T[i, j] for i in range(j, 4)]) for k, j in FULL}
    columns = [cascade_source(p, q, [C[k, j] for k in range(4)], T[3, j]) for j in range(4)]
    C = {(k, j): columns[j][k] for k, j in FULL}
    w = cascade_source(p, q, w, t[3])
    B = cascade_lower(p, q, B)
    return A, u, B, C, w


def line_scan(groups, blocks_ref, state_ref, map_ref, f_ref, b_ref):
    count, width = blocks_ref.shape[0], 128 // groups
    eights = count // 8
    row = lax.broadcasted_iota(jnp.int32, (8, 128), 0)
    group = lax.broadcasted_iota(jnp.int32, (8, 128), 1) // width

    def moved(x, by):
        by = by * width % 128
        return pltpu.roll(x, by, 1) if by else x

    def value(n):
        parts = [moved(blocks_ref[8 * g : 8 * g + 8, n // groups // 2, n // groups % 2, :], g - n % groups) for g in range(eights)]
        x = parts[0]
        for g in range(1, eights):
            x = jnp.where(group == g, parts[g], x)
        return x

    v = [value(37 + n) for n in range(4)]
    below = pltpu.roll(v[3], 1, 0)
    below = jnp.where(row == 0, jnp.where(group == 0, 0.0, moved(below, 1)), below)
    above = pltpu.roll(v[0], 7, 0)
    above = jnp.where(row == 7, jnp.where(group == eights - 1, 0.0, moved(above, -1)), above)
    inverse = -1.0 / value(43)
    first, last = (
        jnp.exp((1.0 + edge_slope * jnp.abs(gradient)) * inverse) for gradient in (0.5 * (v[1] - below), 0.5 * (above - v[2]))
    )
    block = with_ends(unpack(value), first, last, value(41), value(42))
    for n, x in enumerate(pack(block)):
        map_ref[n] = x

    def block_at(m):
        return unpack(lambda n: map_ref[n, m : m + 1, :])

    for reach in (1, 2, 4):
        other = tuple(
            {key: pltpu.roll(x, 8 - reach, 0) for key, x in part.items()} if isinstance(part, dict) else [pltpu.roll(x, 8 - reach, 0) for x in part]
            for part in block
        )
        block = compose(block, other)
    joined = unpack(lambda n, values=pack(block): values[n][0:1])

    here = group[0:1]
    zero = [jnp.zeros((1, 128), jnp.float32)] * 4
    f = zero
    for g in range(1, eights):
        through = [moved(x, 1) for x in forward_out(joined, f)]
        f = [jnp.where(here == g, x, y) for x, y in zip(through, f)]
    b = zero
    for g in reversed(range(eights - 1)):
        through = [moved(x, -1) for x in backward_out(joined, f, b)]
        b = [jnp.where(here == g, x, y) for x, y in zip(through, b)]

    inside = []
    for m in range(8):
        for k in range(4):
            f_ref[k, m : m + 1, :] = f[k]
        inside.append(f)
        f = forward_out(block_at(m), f)
    for m in reversed(range(8)):
        for k in range(4):
            b_ref[k, m : m + 1, :] = b[k]
        b = backward_out(block_at(m), inside[m], b)

    back = [f_ref[k] for k in range(4)] + [b_ref[k] for k in range(4)] + [first, last]
    for g in range(eights):
        some = slice(8 * g, 8 * g + 8)
        for start in range(0, 10, groups):
            x = moved(back[start], -g)
            for n in range(1, min(groups, 10 - start)):
                x = jnp.where(group == n, moved(back[start + n], n - g), x)
            state_ref[some, start // groups, :] = x
    for r in range(-(-10 // groups), state_ref.shape[1]):
        state_ref[:, r, :] = jnp.zeros((count, 128), jnp.float32)


def plane_scan(reach_ref, blocks_ref, state_ref, map_ref, f_ref, b_ref):
    count = blocks_ref.shape[0]
    row = lax.broadcasted_iota(jnp.int32, (count, 128), 0)
    value = lambda n, some=slice(None): blocks_ref[some, n // 4, n % 4, :]
    v = [value(37 + n) for n in range(4)]
    below = jnp.where(row == 0, 0.0, pltpu.roll(v[3], 1, 0))
    above = jnp.where(row == count - 1, 0.0, pltpu.roll(v[0], count - 1, 0))
    here = blocks_ref[0, 10, 3:4, :]
    reach = reach_ref[0:1, :]
    for at in range(count):
        reach = jnp.where(here == float(at), reach_ref[at % 4 : at % 4 + 1, :], reach)
    inverse = -1.0 / reach
    for n, gradient in enumerate((0.5 * (v[1] - below), 0.5 * (above - v[2]))):
        map_ref[37 + n] = jnp.exp((1.0 + edge_slope * jnp.abs(gradient)) * inverse)
    for start in range(0, count, 8):
        some = slice(start, start + 8)
        block = unpack(lambda n: value(n, some))
        block = with_ends(block, map_ref[37, some, :], map_ref[38, some, :], value(41, some), value(42, some))
        for n, x in enumerate(pack(block)):
            map_ref[n, some, :] = x

    def block_at(m):
        return unpack(lambda n: map_ref[n, m : m + 1, :])

    f = [jnp.zeros((1, 128), jnp.float32)] * 4
    for m in range(count):
        for k in range(4):
            f_ref[k, m : m + 1, :] = f[k]
        f = forward_out(block_at(m), f)
    b = [jnp.zeros((1, 128), jnp.float32)] * 4
    for m in reversed(range(count)):
        for k in range(4):
            b_ref[k, m : m + 1, :] = b[k]
        b = backward_out(block_at(m), [f_ref[k, m : m + 1, :] for k in range(4)], b)

    here = jnp.broadcast_to(here, (4, 128))

    def mine(at):
        x = at(0)
        for g in range(1, count // 4):
            x = jnp.where(here > 4 * g - 0.5, at(g), x)
        return x

    for k in range(4):
        state_ref[:, k, :] = mine(lambda g: f_ref[k, 4 * g : 4 * g + 4, :])
        state_ref[:, 4 + k, :] = mine(lambda g: b_ref[k, 4 * g : 4 * g + 4, :])
    for n in range(2):
        state_ref[:, 8 + n, :] = mine(lambda g: map_ref[37 + n, 4 * g : 4 * g + 4, :])
    for n in range(10, 16):
        state_ref[:, n, :] = jnp.zeros((4, 128), jnp.float32)


f32 = lambda *shape: jax.ShapeDtypeStruct(shape, jnp.float32)
vmem = lambda *shape: pltpu.VMEM(shape, jnp.float32)
plane = (512, 128)


def call(kernel, out_shape, scratch, *operands):
    return pl.pallas_call(kernel, out_shape=out_shape, scratch_shapes=scratch, compiler_params=params)(*operands)


def states(chunks, axis):
    size = lax.axis_size(axis)
    groups = size // 4
    chunks = lax.all_to_all(chunks, axis, 0, 0, tiled=True)
    scratch = [vmem(37, 8, 128), vmem(4, 8, 128), vmem(4, 8, 128)]
    entering = call(functools.partial(line_scan, groups), f32(size, 16 // groups, 128), scratch, chunks)
    return lax.all_to_all(entering, axis, 0, 0, tiled=True)


def states_by_planes(chunks, axis, reach):
    size = lax.axis_size(axis)
    blocks = lax.all_to_all(chunks, axis, 0, 0, tiled=True)
    entering = call(plane_scan, f32(4, 16, 128), [vmem(39, size, 128), vmem(4, size, 128), vmem(4, size, 128)], reach, blocks)
    fours = [[4 * g + i for i in range(4)] for g in range(size // 4)]
    return lax.all_to_all(entering, axis, 0, 0, axis_index_groups=fours, tiled=True)


def per_device(intensity, reach_along_x, reach_along_y):
    def maps(axis):
        size = lax.axis_size(axis)
        return [f32(*padded), f32(37, 8, 128), f32(size, 11, 4, 128) if axis == "gy" else f32(size, SLOTS * 2 // size, 2, 128)]


    work = [vmem(SLOTS * APART, 128)]
    ending = [vmem(*padded), vmem(STEPS, 8, 128), vmem(*padded), vmem(8 * APART, 128)]
    vt, y_reach, source, dx, x_half, x_chunks = call(
        x_first, [f32(*plane), f32(4, 128), f32(*padded)] + maps("gx"), [vmem(4, 128)] + work,
        jnp.concatenate([intensity.reshape(plane), reach_along_x, reach_along_y]),
    )
    x_states = states(x_chunks, "gx")
    t, dy, y_half, y_chunks = call(
        x_second_y_first, [f32(*padded)] + maps("gy"), ending + work, vt, y_reach, source, dx, x_half, x_states
    )
    y_states = states_by_planes(y_chunks, "gy", y_reach)
    out = call(y_second, f32(*plane), ending, t, dy, y_half, y_states)
    return out.reshape(4, 128, 128)


def solution(mesh):
    return jax.shard_map(
        per_device,
        mesh=mesh,
        in_specs=(P(None, "gx", "gy"), P(None, "gy"), P(None, "gx")),
        out_specs=P(None, "gx", "gy"),
        check_vma=False,
    )
```

```python
import functools

import jax
import jax.numpy as jnp
from jax import lax
from jax.experimental import pallas as pl
from jax.experimental.pallas import tpu as pltpu
from jax.sharding import PartitionSpec as P

edge_slope = 3.0

LOWER = [(k, j) for k in range(4) for j in range(k + 1)]
BELOW = [(k, j) for k in range(4) for j in range(k)]
FULL = [(k, j) for k in range(4) for j in range(4)]
VALUES = 37

params = pltpu.CompilerParams(vmem_limit_bytes=48 * 1024 * 1024)
MATRICES = 29
SLOTS = 48
APART = 9


def unpack_matrices(get):
    A, B = {}, {}
    for n, kj in enumerate(BELOW):
        A[kj], B[kj] = get(1 + n), get(7 + n)
    power = get(0)
    for k in range(4):
        A[k, k] = B[k, k] = power
        power = power * power
    return A, B, {kj: get(13 + n) for n, kj in enumerate(FULL)}


def pack_matrices(matrices):
    A, B, C = matrices
    return [A[0, 0]] + [A[kj] for kj in BELOW] + [B[kj] for kj in BELOW] + [C[kj] for kj in FULL]


def unpack(get):
    A, B, C = unpack_matrices(get)
    vectors = [get(MATRICES + n) for n in range(8)]
    return A, vectors[:4], B, C, vectors[4:]


def pack(block):
    A, u, B, C, w = block
    return pack_matrices((A, B, C)) + list(u) + list(w)


def total(terms):
    terms = list(terms)
    while len(terms) > 1:
        terms = [a + b for a, b in zip(terms[::2], terms[1::2])] + terms[len(terms) - len(terms) % 2 :]
    return terms[0]


def lower_times(M, x):
    return [total([M[k, j] * x[j] for j in range(k + 1)]) for k in range(4)]


def full_times(M, x):
    return [total([M[k, j] * x[j] for j in range(4)]) for k in range(4)]


def plus(x, y):
    return [a + b for a, b in zip(x, y)]


def lower_product(M, N):
    return {(k, j): total([M[k, i] * N[i, j] for i in range(j, k + 1)]) for k, j in LOWER}


def compose_matrices(left, right):
    A1, B1, C1 = left
    A2, B2, C2 = right
    A = lower_product(A2, A1)
    B = lower_product(B1, B2)
    CA = {(k, j): total([C2[k, i] * A1[i, j] for i in range(j, 4)]) for k, j in FULL}
    C = {(k, j): total([B1[k, i] * CA[i, j] for i in range(k + 1)]) + C1[k, j] for k, j in FULL}
    return A, B, C


def compose_vectors(B1, A2, C2, left, right):
    u1, w1 = left
    u2, w2 = right
    u = plus(lower_times(A2, u1), u2)
    w = plus(lower_times(B1, plus(full_times(C2, u1), w2)), w1)
    return u, w


def compose(left, right):
    A1, u1, B1, C1, w1 = left
    A2, u2, B2, C2, w2 = right
    A, B, C = compose_matrices((A1, B1, C1), (A2, B2, C2))
    u, w = compose_vectors(B1, A2, C2, (u1, w1), (u2, w2))
    return A, u, B, C, w


def forward_out(block, f):
    A, u = block[:2]
    return [total([A[k, j] * f[j] for j in range(k + 1)] + [u[k]]) for k in range(4)]


def backward_out(block, f, b):
    B, C, w = block[2:]
    return [total([B[k, j] * b[j] for j in range(k + 1)] + [C[k, j] * f[j] for j in range(4)] + [w[k]]) for k in range(4)]


def poles_of(d):
    p = [d]
    for _ in range(3):
        p.append(p[-1] * p[-1])
    return p, [1.0 - x for x in p]


STEPS, UNROLL = 64, 16
PITCH = 65
padded = (8 * PITCH, 128)


def loop(body, carry, reverse=False, unroll=UNROLL):
    def some(n, carry):
        for k in range(unroll):
            at = n * unroll + k
            carry = body(STEPS - 1 - at if reverse else at, carry)
        return carry

    return some(0, carry) if unroll == STEPS else lax.fori_loop(0, STEPS // unroll, some, carry)


def rows(s):
    return pl.ds(s, 8, stride=PITCH)


def decay_block(v, inverse):
    at = lax.broadcasted_iota(jnp.int32, v.shape, 0)
    n = v.shape[0]
    gradient = 0.5 * (pltpu.roll(v, n - 1, 0) - pltpu.roll(v, 1, 0))
    d = jnp.exp((1.0 + edge_slope * jnp.abs(gradient)) * inverse)
    return jnp.where((at == 0) | (at == n - 1), 1.0, d)


def cascade_lower(p, q, M):
    M = dict(M)
    for j in range(4):
        M[j, j] = p[j] * M[j, j]
        for k in range(j + 1, 4):
            M[k, j] = p[k] * M[k, j] + q[k] * M[k - 1, j]
    return M


def cascade_source(p, q, x, source):
    x = list(x)
    for k in range(4):
        x[k] = p[k] * x[k] + q[k] * (source if k == 0 else x[k - 1])
    return x


def before_step(p, q, B):
    new, inner = {}, []
    for k in range(4):
        carried = B[k, k]
        new[k, k] = p[k] * carried
        for j in reversed(range(k)):
            carried = B[k, j] + q[j + 1] * carried
            new[k, j] = p[j] * carried
        inner.append(q[0] * carried)
    return new, inner


def half_maps(v_ref, d_ref):
    one, zero = jnp.ones((8, 128), jnp.float32), jnp.zeros((8, 128), jnp.float32)

    def step(s, carry):
        A, u, B, C, w = carry
        A, B = dict(zip(LOWER, A)), dict(zip(LOWER, B))
        p, q = poles_of(d_ref[rows(s), :])
        u = cascade_source(p, q, u, v_ref[rows(s), :])
        A = cascade_lower(p, q, A)
        B, inner = before_step(p, q, B)
        C = [c + inner[k] * A[3, j] for c, (k, j) in zip(C, FULL)]
        w = [x + y * u[3] for x, y in zip(w, inner)]
        return [A[kj] for kj in LOWER], u, [B[kj] for kj in LOWER], C, w

    start = [one if k == j else zero for k, j in LOWER]
    A, u, B, C, w = loop(step, (start, [zero] * 4, start, [zero] * 16, [zero] * 4))
    return dict(zip(LOWER, A)), u, dict(zip(LOWER, B)), dict(zip(FULL, C)), w


def after(part):
    if isinstance(part, dict):
        return {key: pltpu.roll(x, 7, 0) for key, x in part.items()}
    return [pltpu.roll(x, 7, 0) for x in part]


def planes():
    return [slice(z * 128, (z + 1) * 128) for z in range(4)]


def place(i):
    return pl.ds(i // STEPS * PITCH + i % STEPS, 4, stride=2 * PITCH)


def spread(ref, z, block):
    for h in range(2):
        at = (2 * z + h) * PITCH
        ref[at : at + STEPS, :] = block[h * STEPS : (h + 1) * STEPS]


def gather(ref, z):
    at = 2 * z * PITCH
    return jnp.concatenate([ref[at : at + STEPS, :], ref[at + PITCH : at + PITCH + STEPS, :]], axis=0)


def swap(x, groups):
    row, lane = (lax.broadcasted_iota(jnp.int32, x.shape, axis) for axis in range(2))
    width = 128 // groups
    t = 1
    while t < groups:
        lower, right = (row // t) % 2 == 1, (lane // (width * t)) % 2 == 1
        up = pltpu.roll(pltpu.roll(x, 8 - t, 0), width * t, 1)
        down = pltpu.roll(pltpu.roll(x, t, 0), 128 - width * t, 1)
        x = jnp.where(lower == right, x, jnp.where(lower, down, up))
        t *= 2
    return x


def summarise(v_ref, source_ref, reach_ref, d_ref, half_ref, chunks_ref, pair_ref):
    for z, here in enumerate(planes()):
        spread(d_ref, z, decay_block(v_ref[here, :], -1.0 / reach_ref[z : z + 1, :]))
    block = half_maps(source_ref, d_ref)
    for n, value in enumerate(pack(block)):
        half_ref[n] = value
    for n, value in enumerate(pack(compose(block, tuple(after(part) for part in block)))):
        pair_ref[n * APART : n * APART + 8, :] = value
    ends = [v_ref[pl.ds(i, 4, stride=128), :] for i in (0, 1, 126, 127)] + [source_ref[place(0), :], source_ref[place(127), :], reach_ref[...]]
    for n, value in enumerate(ends):
        pair_ref[pl.ds((37 + n) * APART, 4, stride=2), :] = value
    for n in range(44, SLOTS):
        pair_ref[n * APART : n * APART + 8, :] = jnp.zeros((8, 128), jnp.float32)
    if chunks_ref.shape[2] == 4:
        row = lax.broadcasted_iota(jnp.int32, (4, 128), 0)
        for z in range(4):
            for n in range(0, 44, 4):
                x = pair_ref[pl.ds(n * APART + 2 * z, 4, stride=APART), :]
                for at in range(z, chunks_ref.shape[0], 4):
                    chunks_ref[at, n // 4] = x if n != 40 else jnp.where(row == 3, float(at), x)
        return
    per_plane = chunks_ref.shape[0] // 4
    groups = per_plane
    for z in range(4):
        chunks = slice(z * per_plane, (z + 1) * per_plane)
        for n in range(0, SLOTS, 8):
            x = swap(pair_ref[pl.ds(n * APART + 2 * z, 8, stride=APART), :], groups)
            for a in range(8 // groups):
                r = n // groups + a
                chunks_ref[chunks, r // 2, r % 2, :] = x[a * groups : (a + 1) * groups]


def finish(v_ref, half_ref, state_ref, d_ref, c_ref, out_ref, wide_ref):
    groups = state_ref.shape[0] // 4
    for z in range(4):
        chunks = slice(z * groups, (z + 1) * groups)
        if groups == 1:
            x, ends = state_ref[z, 0:8, :], state_ref[z, 8:16, :]
        else:
            count = 8 // groups
            x = swap(jnp.concatenate([state_ref[chunks, a, :] for a in range(count)], axis=0), groups)
            ends = swap(jnp.concatenate([state_ref[chunks, count, :]] * count, axis=0), groups)
        wide_ref[pl.ds(2 * z, 8, stride=APART), :] = x
        wide_ref[pl.ds(2 * z + 1, 8, stride=APART), :] = x
        first, last = 2 * z * PITCH, (2 * z + 1) * PITCH + STEPS - 1
        d_ref[first : first + 1, :] = ends[0:1]
        d_ref[last : last + 1, :] = ends[1:2]
    f = [wide_ref[k * APART : k * APART + 8, :] for k in range(4)]
    b = [wide_ref[k * APART : k * APART + 8, :] for k in range(4, 8)]
    block = unpack(lambda n: half_ref[n])
    second = lax.broadcasted_iota(jnp.int32, (8, 128), 0) % 2 == 1
    p, q = poles_of(d_ref[rows(0), :])
    f_middle = [pltpu.roll(x, 1, 0) for x in forward_out(block, cascade_source(p, q, f, v_ref[rows(0), :]))]
    p, q = poles_of(d_ref[rows(STEPS - 1), :])
    f_last = cascade_source(p, q, forward_out(block, f_middle), v_ref[rows(STEPS - 1), :])
    b_middle = [pltpu.roll(x, 7, 0) for x in backward_out(block, f_middle, cascade_source(p, q, b, f_last[3]))]
    f = [jnp.where(second, x, y) for x, y in zip(f_middle, f)]
    b = [jnp.where(second, y, x) for x, y in zip(b_middle, b)]

    def forward(s, f):
        p, q = poles_of(d_ref[rows(s), :])
        f = cascade_source(p, q, f, v_ref[rows(s), :])
        c_ref[s] = f[3]
        return f

    loop(forward, f, unroll=STEPS)

    def backward(s, b):
        p, q = poles_of(d_ref[rows(s), :])
        b = cascade_source(p, q, b, c_ref[s])
        out_ref[rows(s), :] = b[3]
        return b

    loop(backward, b, reverse=True, unroll=STEPS)


def x_first(arguments_ref, vt_ref, y_reach_ref, source_ref, d_ref, half_ref, chunks_ref, reach_ref, pair_ref):
    for z, here in enumerate(planes()):
        vt_ref[here, :] = arguments_ref[here, :].T
        spread(source_ref, z, arguments_ref[here, :])
    reach_ref[...] = arguments_ref[512:516, :]
    y_reach_ref[...] = arguments_ref[516:520, :]
    summarise(arguments_ref, source_ref, reach_ref, d_ref, half_ref, chunks_ref, pair_ref)


def x_second_y_first(
    vt_ref, reach_ref, source_ref, dx_ref, xhalf_ref, state_ref,
    t_ref, d_ref, half_ref, chunks_ref,
    ends_ref, c_ref, across_ref, wide_ref, pair_ref,
):
    ends_ref[...] = dx_ref[...]
    finish(source_ref, xhalf_ref, state_ref, ends_ref, c_ref, across_ref, wide_ref)
    for z in range(4):
        spread(t_ref, z, gather(across_ref, z).T)
    summarise(vt_ref, t_ref, reach_ref, d_ref, half_ref, chunks_ref, pair_ref)


def y_second(t_ref, d_ref, half_ref, state_ref, out_ref, ends_ref, c_ref, done_ref, wide_ref):
    ends_ref[...] = d_ref[...]
    finish(t_ref, half_ref, state_ref, ends_ref, c_ref, done_ref, wide_ref)
    for z, here in enumerate(planes()):
        out_ref[here, :] = gather(done_ref, z).T


def with_ends(block, first, last, source_first, source_last):
    A, u, B, C, w = block
    one, zero = jnp.ones_like(first), jnp.zeros_like(first)
    identity = {(k, j): one if k == j else zero for k, j in LOWER}
    p, q = poles_of(last)
    A, u = cascade_lower(p, q, A), cascade_source(p, q, u, source_last)
    inner = lower_times(B, cascade_source(p, q, [zero] * 4, one))
    B = lower_product(B, cascade_lower(p, q, identity))
    C = {(k, j): C[k, j] + inner[k] * A[3, j] for k, j in FULL}
    w = [x + y * u[3] for x, y in zip(w, inner)]
    p, q = poles_of(first)
    T, t = cascade_lower(p, q, identity), cascade_source(p, q, [zero] * 4, source_first)
    w = plus(w, full_times(C, t))
    u = plus(u, lower_times(A, t))
    A = lower_product(A, T)
    C = {(k, j): total([C[k, i] * T[i, j] for i in range(j, 4)]) for k, j in FULL}
    columns = [cascade_source(p, q, [C[k, j] for k in range(4)], T[3, j]) for j in range(4)]
    C = {(k, j): columns[j][k] for k, j in FULL}
    w = cascade_source(p, q, w, t[3])
    B = cascade_lower(p, q, B)
    return A, u, B, C, w


def line_scan(groups, blocks_ref, state_ref, map_ref, f_ref, b_ref):
    count, width = blocks_ref.shape[0], 128 // groups
    eights = count // 8
    row = lax.broadcasted_iota(jnp.int32, (8, 128), 0)
    group = lax.broadcasted_iota(jnp.int32, (8, 128), 1) // width

    def moved(x, by):
        by = by * width % 128
        return pltpu.roll(x, by, 1) if by else x

    def value(n):
        parts = [moved(blocks_ref[8 * g : 8 * g + 8, n // groups // 2, n // groups % 2, :], g - n % groups) for g in range(eights)]
        x = parts[0]
        for g in range(1, eights):
            x = jnp.where(group == g, parts[g], x)
        return x

    v = [value(37 + n) for n in range(4)]
    below = pltpu.roll(v[3], 1, 0)
    below = jnp.where(row == 0, jnp.where(group == 0, 0.0, moved(below, 1)), below)
    above = pltpu.roll(v[0], 7, 0)
    above = jnp.where(row == 7, jnp.where(group == eights - 1, 0.0, moved(above, -1)), above)
    inverse = -1.0 / value(43)
    first, last = (
        jnp.exp((1.0 + edge_slope * jnp.abs(gradient)) * inverse) for gradient in (0.5 * (v[1] - below), 0.5 * (above - v[2]))
    )
    block = with_ends(unpack(value), first, last, value(41), value(42))
    for n, x in enumerate(pack(block)):
        map_ref[n] = x

    def block_at(m):
        return unpack(lambda n: map_ref[n, m : m + 1, :])

    for reach in (1, 2, 4):
        other = tuple(
            {key: pltpu.roll(x, 8 - reach, 0) for key, x in part.items()} if isinstance(part, dict) else [pltpu.roll(x, 8 - reach, 0) for x in part]
            for part in block
        )
        block = compose(block, other)
    joined = unpack(lambda n, values=pack(block): values[n][0:1])

    here = group[0:1]
    zero = [jnp.zeros((1, 128), jnp.float32)] * 4
    f = zero
    for g in range(1, eights):
        through = [moved(x, 1) for x in forward_out(joined, f)]
        f = [jnp.where(here == g, x, y) for x, y in zip(through, f)]
    b = zero
    for g in reversed(range(eights - 1)):
        through = [moved(x, -1) for x in backward_out(joined, f, b)]
        b = [jnp.where(here == g, x, y) for x, y in zip(through, b)]

    inside = []
    for m in range(8):
        for k in range(4):
            f_ref[k, m : m + 1, :] = f[k]
        inside.append(f)
        f = forward_out(block_at(m), f)
    for m in reversed(range(8)):
        for k in range(4):
            b_ref[k, m : m + 1, :] = b[k]
        b = backward_out(block_at(m), inside[m], b)

    back = [f_ref[k] for k in range(4)] + [b_ref[k] for k in range(4)] + [first, last]
    for g in range(eights):
        some = slice(8 * g, 8 * g + 8)
        for start in range(0, 10, groups):
            x = moved(back[start], -g)
            for n in range(1, min(groups, 10 - start)):
                x = jnp.where(group == n, moved(back[start + n], n - g), x)
            state_ref[some, start // groups, :] = x
    for r in range(-(-10 // groups), state_ref.shape[1]):
        state_ref[:, r, :] = jnp.zeros((count, 128), jnp.float32)


def plane_scan(reach_ref, blocks_ref, state_ref, map_ref, f_ref, b_ref):
    count = blocks_ref.shape[0]
    row = lax.broadcasted_iota(jnp.int32, (count, 128), 0)
    value = lambda n, some=slice(None): blocks_ref[some, n // 4, n % 4, :]
    v = [value(37 + n) for n in range(4)]
    below = jnp.where(row == 0, 0.0, pltpu.roll(v[3], 1, 0))
    above = jnp.where(row == count - 1, 0.0, pltpu.roll(v[0], count - 1, 0))
    here = blocks_ref[0, 10, 3:4, :]
    reach = reach_ref[0:1, :]
    for at in range(count):
        reach = jnp.where(here == float(at), reach_ref[at % 4 : at % 4 + 1, :], reach)
    inverse = -1.0 / reach
    for n, gradient in enumerate((0.5 * (v[1] - below), 0.5 * (above - v[2]))):
        map_ref[37 + n] = jnp.exp((1.0 + edge_slope * jnp.abs(gradient)) * inverse)
    for start in range(0, count, 8):
        some = slice(start, start + 8)
        block = unpack(lambda n: value(n, some))
        block = with_ends(block, map_ref[37, some, :], map_ref[38, some, :], value(41, some), value(42, some))
        for n, x in enumerate(pack(block)):
            map_ref[n, some, :] = x

    def block_at(m):
        return unpack(lambda n: map_ref[n, m : m + 1, :])

    f = [jnp.zeros((1, 128), jnp.float32)] * 4
    for m in range(count):
        for k in range(4):
            f_ref[k, m : m + 1, :] = f[k]
        f = forward_out(block_at(m), f)
    b = [jnp.zeros((1, 128), jnp.float32)] * 4
    for m in reversed(range(count)):
        for k in range(4):
            b_ref[k, m : m + 1, :] = b[k]
        b = backward_out(block_at(m), [f_ref[k, m : m + 1, :] for k in range(4)], b)

    here = jnp.broadcast_to(here, (4, 128))

    def mine(at):
        x = at(0)
        for g in range(1, count // 4):
            x = jnp.where(here > 4 * g - 0.5, at(g), x)
        return x

    for k in range(4):
        state_ref[:, k, :] = mine(lambda g: f_ref[k, 4 * g : 4 * g + 4, :])
        state_ref[:, 4 + k, :] = mine(lambda g: b_ref[k, 4 * g : 4 * g + 4, :])
    for n in range(2):
        state_ref[:, 8 + n, :] = mine(lambda g: map_ref[37 + n, 4 * g : 4 * g + 4, :])
    for n in range(10, 16):
        state_ref[:, n, :] = jnp.zeros((4, 128), jnp.float32)


f32 = lambda *shape: jax.ShapeDtypeStruct(shape, jnp.float32)
vmem = lambda *shape: pltpu.VMEM(shape, jnp.float32)
plane = (512, 128)


def call(kernel, out_shape, scratch, *operands):
    return pl.pallas_call(kernel, out_shape=out_shape, scratch_shapes=scratch, compiler_params=params)(*operands)


def states(chunks, axis):
    size = lax.axis_size(axis)
    groups = size // 4
    chunks = lax.all_to_all(chunks, axis, 0, 0, tiled=True)
    scratch = [vmem(37, 8, 128), vmem(4, 8, 128), vmem(4, 8, 128)]
    entering = call(functools.partial(line_scan, groups), f32(size, 16 // groups, 128), scratch, chunks)
    return lax.all_to_all(entering, axis, 0, 0, tiled=True)


def states_by_planes(chunks, axis, reach):
    size = lax.axis_size(axis)
    blocks = lax.all_to_all(chunks, axis, 0, 0, tiled=True)
    entering = call(plane_scan, f32(4, 16, 128), [vmem(39, size, 128), vmem(4, size, 128), vmem(4, size, 128)], reach, blocks)
    fours = [[4 * g + i for i in range(4)] for g in range(size // 4)]
    return lax.all_to_all(entering, axis, 0, 0, axis_index_groups=fours, tiled=True)


def per_device(intensity, reach_along_x, reach_along_y):
    def maps(axis):
        size = lax.axis_size(axis)
        return [f32(*padded), f32(37, 8, 128), f32(size, 11, 4, 128) if axis == "gy" else f32(size, SLOTS * 2 // size, 2, 128)]


    work = [vmem(SLOTS * APART, 128)]
    ending = [vmem(*padded), vmem(STEPS, 8, 128), vmem(*padded), vmem(8 * APART, 128)]
    vt, y_reach, source, dx, x_half, x_chunks = call(
        x_first, [f32(*plane), f32(4, 128), f32(*padded)] + maps("gx"), [vmem(4, 128)] + work,
        jnp.concatenate([intensity.reshape(plane), reach_along_x, reach_along_y]),
    )
    x_states = states(x_chunks, "gx")
    t, dy, y_half, y_chunks = call(
        x_second_y_first, [f32(*padded)] + maps("gy"), ending + work, vt, y_reach, source, dx, x_half, x_states
    )
    y_states = states_by_planes(y_chunks, "gy", y_reach)
    out = call(y_second, f32(*plane), ending, t, dy, y_half, y_states)
    return out.reshape(4, 128, 128)


def solution(mesh):
    return jax.shard_map(
        per_device,
        mesh=mesh,
        in_specs=(P(None, "gx", "gy"), P(None, "gy"), P(None, "gx")),
        out_specs=P(None, "gx", "gy"),
        check_vma=False,
    )
```

```python
import functools

import jax
import jax.numpy as jnp
from jax import lax
from jax.experimental import pallas as pl
from jax.experimental.pallas import tpu as pltpu
from jax.sharding import PartitionSpec as P

edge_slope = 3.0

LOWER = [(k, j) for k in range(4) for j in range(k + 1)]
BELOW = [(k, j) for k in range(4) for j in range(k)]
FULL = [(k, j) for k in range(4) for j in range(4)]
VALUES = 37

params = pltpu.CompilerParams(vmem_limit_bytes=48 * 1024 * 1024)
MATRICES = 29
SLOTS = 48
APART = 9


def unpack_matrices(get):
    A, B = {}, {}
    for n, kj in enumerate(BELOW):
        A[kj], B[kj] = get(1 + n), get(7 + n)
    power = get(0)
    for k in range(4):
        A[k, k] = B[k, k] = power
        power = power * power
    return A, B, {kj: get(13 + n) for n, kj in enumerate(FULL)}


def pack_matrices(matrices):
    A, B, C = matrices
    return [A[0, 0]] + [A[kj] for kj in BELOW] + [B[kj] for kj in BELOW] + [C[kj] for kj in FULL]


def unpack(get):
    A, B, C = unpack_matrices(get)
    vectors = [get(MATRICES + n) for n in range(8)]
    return A, vectors[:4], B, C, vectors[4:]


def pack(block):
    A, u, B, C, w = block
    return pack_matrices((A, B, C)) + list(u) + list(w)


def total(terms):
    terms = list(terms)
    while len(terms) > 1:
        terms = [a + b for a, b in zip(terms[::2], terms[1::2])] + terms[len(terms) - len(terms) % 2 :]
    return terms[0]


def lower_times(M, x):
    return [total([M[k, j] * x[j] for j in range(k + 1)]) for k in range(4)]


def full_times(M, x):
    return [total([M[k, j] * x[j] for j in range(4)]) for k in range(4)]


def plus(x, y):
    return [a + b for a, b in zip(x, y)]


def lower_product(M, N):
    return {(k, j): total([M[k, i] * N[i, j] for i in range(j, k + 1)]) for k, j in LOWER}


def compose_matrices(left, right):
    A1, B1, C1 = left
    A2, B2, C2 = right
    A = lower_product(A2, A1)
    B = lower_product(B1, B2)
    CA = {(k, j): total([C2[k, i] * A1[i, j] for i in range(j, 4)]) for k, j in FULL}
    C = {(k, j): total([B1[k, i] * CA[i, j] for i in range(k + 1)]) + C1[k, j] for k, j in FULL}
    return A, B, C


def compose_vectors(B1, A2, C2, left, right):
    u1, w1 = left
    u2, w2 = right
    u = plus(lower_times(A2, u1), u2)
    w = plus(lower_times(B1, plus(full_times(C2, u1), w2)), w1)
    return u, w


def compose(left, right):
    A1, u1, B1, C1, w1 = left
    A2, u2, B2, C2, w2 = right
    A, B, C = compose_matrices((A1, B1, C1), (A2, B2, C2))
    u, w = compose_vectors(B1, A2, C2, (u1, w1), (u2, w2))
    return A, u, B, C, w


def forward_out(block, f):
    A, u = block[:2]
    return [total([A[k, j] * f[j] for j in range(k + 1)] + [u[k]]) for k in range(4)]


def backward_out(block, f, b):
    B, C, w = block[2:]
    return [total([B[k, j] * b[j] for j in range(k + 1)] + [C[k, j] * f[j] for j in range(4)] + [w[k]]) for k in range(4)]


def poles_of(d):
    p = [d]
    for _ in range(3):
        p.append(p[-1] * p[-1])
    return p, [1.0 - x for x in p]


STEPS, UNROLL = 64, 32
PITCH = 65
padded = (8 * PITCH, 128)


def loop(body, carry, reverse=False, unroll=UNROLL):
    def some(n, carry):
        for k in range(unroll):
            at = n * unroll + k
            carry = body(STEPS - 1 - at if reverse else at, carry)
        return carry

    return some(0, carry) if unroll == STEPS else lax.fori_loop(0, STEPS // unroll, some, carry)


def rows(s):
    return pl.ds(s, 8, stride=PITCH)


def decay_block(v, inverse):
    at = lax.broadcasted_iota(jnp.int32, v.shape, 0)
    n = v.shape[0]
    gradient = 0.5 * (pltpu.roll(v, n - 1, 0) - pltpu.roll(v, 1, 0))
    d = jnp.exp((1.0 + edge_slope * jnp.abs(gradient)) * inverse)
    return jnp.where((at == 0) | (at == n - 1), 1.0, d)


def cascade_lower(p, q, M):
    M = dict(M)
    for j in range(4):
        M[j, j] = p[j] * M[j, j]
        for k in range(j + 1, 4):
            M[k, j] = p[k] * M[k, j] + q[k] * M[k - 1, j]
    return M


def cascade_source(p, q, x, source):
    x = list(x)
    for k in range(4):
        x[k] = p[k] * x[k] + q[k] * (source if k == 0 else x[k - 1])
    return x


def before_step(p, q, B):
    new, inner = {}, []
    for k in range(4):
        carried = B[k, k]
        new[k, k] = p[k] * carried
        for j in reversed(range(k)):
            carried = B[k, j] + q[j + 1] * carried
            new[k, j] = p[j] * carried
        inner.append(q[0] * carried)
    return new, inner


def half_maps(v_ref, d_ref):
    one, zero = jnp.ones((8, 128), jnp.float32), jnp.zeros((8, 128), jnp.float32)

    def step(s, carry):
        A, u, B, C, w = carry
        A, B = dict(zip(LOWER, A)), dict(zip(LOWER, B))
        p, q = poles_of(d_ref[rows(s), :])
        u = cascade_source(p, q, u, v_ref[rows(s), :])
        A = cascade_lower(p, q, A)
        B, inner = before_step(p, q, B)
        C = [c + inner[k] * A[3, j] for c, (k, j) in zip(C, FULL)]
        w = [x + y * u[3] for x, y in zip(w, inner)]
        return [A[kj] for kj in LOWER], u, [B[kj] for kj in LOWER], C, w

    start = [one if k == j else zero for k, j in LOWER]
    A, u, B, C, w = loop(step, (start, [zero] * 4, start, [zero] * 16, [zero] * 4))
    return dict(zip(LOWER, A)), u, dict(zip(LOWER, B)), dict(zip(FULL, C)), w


def after(part):
    if isinstance(part, dict):
        return {key: pltpu.roll(x, 7, 0) for key, x in part.items()}
    return [pltpu.roll(x, 7, 0) for x in part]


def planes():
    return [slice(z * 128, (z + 1) * 128) for z in range(4)]


def place(i):
    return pl.ds(i // STEPS * PITCH + i % STEPS, 4, stride=2 * PITCH)


def spread(ref, z, block):
    for h in range(2):
        at = (2 * z + h) * PITCH
        ref[at : at + STEPS, :] = block[h * STEPS : (h + 1) * STEPS]


def gather(ref, z):
    at = 2 * z * PITCH
    return jnp.concatenate([ref[at : at + STEPS, :], ref[at + PITCH : at + PITCH + STEPS, :]], axis=0)


def swap(x, groups):
    row, lane = (lax.broadcasted_iota(jnp.int32, x.shape, axis) for axis in range(2))
    width = 128 // groups
    t = 1
    while t < groups:
        lower, right = (row // t) % 2 == 1, (lane // (width * t)) % 2 == 1
        up = pltpu.roll(pltpu.roll(x, 8 - t, 0), width * t, 1)
        down = pltpu.roll(pltpu.roll(x, t, 0), 128 - width * t, 1)
        x = jnp.where(lower == right, x, jnp.where(lower, down, up))
        t *= 2
    return x


def summarise(v_ref, source_ref, reach_ref, d_ref, half_ref, chunks_ref, pair_ref):
    for z, here in enumerate(planes()):
        spread(d_ref, z, decay_block(v_ref[here, :], -1.0 / reach_ref[z : z + 1, :]))
    block = half_maps(source_ref, d_ref)
    for n, value in enumerate(pack(block)):
        half_ref[n] = value
    for n, value in enumerate(pack(compose(block, tuple(after(part) for part in block)))):
        pair_ref[n * APART : n * APART + 8, :] = value
    ends = [v_ref[pl.ds(i, 4, stride=128), :] for i in (0, 1, 126, 127)] + [source_ref[place(0), :], source_ref[place(127), :], reach_ref[...]]
    for n, value in enumerate(ends):
        pair_ref[pl.ds((37 + n) * APART, 4, stride=2), :] = value
    for n in range(44, SLOTS):
        pair_ref[n * APART : n * APART + 8, :] = jnp.zeros((8, 128), jnp.float32)
    if chunks_ref.shape[2] == 4:
        row = lax.broadcasted_iota(jnp.int32, (4, 128), 0)
        for z in range(4):
            for n in range(0, 44, 4):
                x = pair_ref[pl.ds(n * APART + 2 * z, 4, stride=APART), :]
                for at in range(z, chunks_ref.shape[0], 4):
                    chunks_ref[at, n // 4] = x if n != 40 else jnp.where(row == 3, float(at), x)
        return
    per_plane = chunks_ref.shape[0] // 4
    groups = per_plane
    for z in range(4):
        chunks = slice(z * per_plane, (z + 1) * per_plane)
        for n in range(0, SLOTS, 8):
            x = swap(pair_ref[pl.ds(n * APART + 2 * z, 8, stride=APART), :], groups)
            for a in range(8 // groups):
                r = n // groups + a
                chunks_ref[chunks, r // 2, r % 2, :] = x[a * groups : (a + 1) * groups]


def finish(v_ref, half_ref, state_ref, d_ref, c_ref, out_ref, wide_ref):
    groups = state_ref.shape[0] // 4
    for z in range(4):
        chunks = slice(z * groups, (z + 1) * groups)
        if groups == 1:
            x, ends = state_ref[z, 0:8, :], state_ref[z, 8:16, :]
        else:
            count = 8 // groups
            x = swap(jnp.concatenate([state_ref[chunks, a, :] for a in range(count)], axis=0), groups)
            ends = swap(jnp.concatenate([state_ref[chunks, count, :]] * count, axis=0), groups)
        wide_ref[pl.ds(2 * z, 8, stride=APART), :] = x
        wide_ref[pl.ds(2 * z + 1, 8, stride=APART), :] = x
        first, last = 2 * z * PITCH, (2 * z + 1) * PITCH + STEPS - 1
        d_ref[first : first + 1, :] = ends[0:1]
        d_ref[last : last + 1, :] = ends[1:2]
    f = [wide_ref[k * APART : k * APART + 8, :] for k in range(4)]
    b = [wide_ref[k * APART : k * APART + 8, :] for k in range(4, 8)]
    block = unpack(lambda n: half_ref[n])
    second = lax.broadcasted_iota(jnp.int32, (8, 128), 0) % 2 == 1
    p, q = poles_of(d_ref[rows(0), :])
    f_middle = [pltpu.roll(x, 1, 0) for x in forward_out(block, cascade_source(p, q, f, v_ref[rows(0), :]))]
    p, q = poles_of(d_ref[rows(STEPS - 1), :])
    f_last = cascade_source(p, q, forward_out(block, f_middle), v_ref[rows(STEPS - 1), :])
    b_middle = [pltpu.roll(x, 7, 0) for x in backward_out(block, f_middle, cascade_source(p, q, b, f_last[3]))]
    f = [jnp.where(second, x, y) for x, y in zip(f_middle, f)]
    b = [jnp.where(second, y, x) for x, y in zip(b_middle, b)]

    def forward(s, f):
        p, q = poles_of(d_ref[rows(s), :])
        f = cascade_source(p, q, f, v_ref[rows(s), :])
        c_ref[s] = f[3]
        return f

    loop(forward, f, unroll=STEPS)

    def backward(s, b):
        p, q = poles_of(d_ref[rows(s), :])
        b = cascade_source(p, q, b, c_ref[s])
        out_ref[rows(s), :] = b[3]
        return b

    loop(backward, b, reverse=True, unroll=STEPS)


def x_first(arguments_ref, vt_ref, y_reach_ref, source_ref, d_ref, half_ref, chunks_ref, reach_ref, pair_ref):
    for z, here in enumerate(planes()):
        vt_ref[here, :] = arguments_ref[here, :].T
        spread(source_ref, z, arguments_ref[here, :])
    reach_ref[...] = arguments_ref[512:516, :]
    y_reach_ref[...] = arguments_ref[516:520, :]
    summarise(arguments_ref, source_ref, reach_ref, d_ref, half_ref, chunks_ref, pair_ref)


def x_second_y_first(
    vt_ref, reach_ref, source_ref, dx_ref, xhalf_ref, state_ref,
    t_ref, d_ref, half_ref, chunks_ref,
    ends_ref, c_ref, across_ref, wide_ref, pair_ref,
):
    ends_ref[...] = dx_ref[...]
    finish(source_ref, xhalf_ref, state_ref, ends_ref, c_ref, across_ref, wide_ref)
    for z in range(4):
        spread(t_ref, z, gather(across_ref, z).T)
    summarise(vt_ref, t_ref, reach_ref, d_ref, half_ref, chunks_ref, pair_ref)


def y_second(t_ref, d_ref, half_ref, state_ref, out_ref, ends_ref, c_ref, done_ref, wide_ref):
    ends_ref[...] = d_ref[...]
    finish(t_ref, half_ref, state_ref, ends_ref, c_ref, done_ref, wide_ref)
    for z, here in enumerate(planes()):
        out_ref[here, :] = gather(done_ref, z).T


def with_ends(block, first, last, source_first, source_last):
    A, u, B, C, w = block
    one, zero = jnp.ones_like(first), jnp.zeros_like(first)
    identity = {(k, j): one if k == j else zero for k, j in LOWER}
    p, q = poles_of(last)
    A, u = cascade_lower(p, q, A), cascade_source(p, q, u, source_last)
    inner = lower_times(B, cascade_source(p, q, [zero] * 4, one))
    B = lower_product(B, cascade_lower(p, q, identity))
    C = {(k, j): C[k, j] + inner[k] * A[3, j] for k, j in FULL}
    w = [x + y * u[3] for x, y in zip(w, inner)]
    p, q = poles_of(first)
    T, t = cascade_lower(p, q, identity), cascade_source(p, q, [zero] * 4, source_first)
    w = plus(w, full_times(C, t))
    u = plus(u, lower_times(A, t))
    A = lower_product(A, T)
    C = {(k, j): total([C[k, i] * T[i, j] for i in range(j, 4)]) for k, j in FULL}
    columns = [cascade_source(p, q, [C[k, j] for k in range(4)], T[3, j]) for j in range(4)]
    C = {(k, j): columns[j][k] for k, j in FULL}
    w = cascade_source(p, q, w, t[3])
    B = cascade_lower(p, q, B)
    return A, u, B, C, w


def line_scan(groups, blocks_ref, state_ref, map_ref, f_ref, b_ref):
    count, width = blocks_ref.shape[0], 128 // groups
    eights = count // 8
    row = lax.broadcasted_iota(jnp.int32, (8, 128), 0)
    group = lax.broadcasted_iota(jnp.int32, (8, 128), 1) // width

    def moved(x, by):
        by = by * width % 128
        return pltpu.roll(x, by, 1) if by else x

    def value(n):
        parts = [moved(blocks_ref[8 * g : 8 * g + 8, n // groups // 2, n // groups % 2, :], g - n % groups) for g in range(eights)]
        x = parts[0]
        for g in range(1, eights):
            x = jnp.where(group == g, parts[g], x)
        return x

    v = [value(37 + n) for n in range(4)]
    below = pltpu.roll(v[3], 1, 0)
    below = jnp.where(row == 0, jnp.where(group == 0, 0.0, moved(below, 1)), below)
    above = pltpu.roll(v[0], 7, 0)
    above = jnp.where(row == 7, jnp.where(group == eights - 1, 0.0, moved(above, -1)), above)
    inverse = -1.0 / value(43)
    first, last = (
        jnp.exp((1.0 + edge_slope * jnp.abs(gradient)) * inverse) for gradient in (0.5 * (v[1] - below), 0.5 * (above - v[2]))
    )
    block = with_ends(unpack(value), first, last, value(41), value(42))
    for n, x in enumerate(pack(block)):
        map_ref[n] = x

    def block_at(m):
        return unpack(lambda n: map_ref[n, m : m + 1, :])

    for reach in (1, 2, 4):
        other = tuple(
            {key: pltpu.roll(x, 8 - reach, 0) for key, x in part.items()} if isinstance(part, dict) else [pltpu.roll(x, 8 - reach, 0) for x in part]
            for part in block
        )
        block = compose(block, other)
    joined = unpack(lambda n, values=pack(block): values[n][0:1])

    here = group[0:1]
    zero = [jnp.zeros((1, 128), jnp.float32)] * 4
    f = zero
    for g in range(1, eights):
        through = [moved(x, 1) for x in forward_out(joined, f)]
        f = [jnp.where(here == g, x, y) for x, y in zip(through, f)]
    b = zero
    for g in reversed(range(eights - 1)):
        through = [moved(x, -1) for x in backward_out(joined, f, b)]
        b = [jnp.where(here == g, x, y) for x, y in zip(through, b)]

    inside = []
    for m in range(8):
        for k in range(4):
            f_ref[k, m : m + 1, :] = f[k]
        inside.append(f)
        f = forward_out(block_at(m), f)
    for m in reversed(range(8)):
        for k in range(4):
            b_ref[k, m : m + 1, :] = b[k]
        b = backward_out(block_at(m), inside[m], b)

    back = [f_ref[k] for k in range(4)] + [b_ref[k] for k in range(4)] + [first, last]
    for g in range(eights):
        some = slice(8 * g, 8 * g + 8)
        for start in range(0, 10, groups):
            x = moved(back[start], -g)
            for n in range(1, min(groups, 10 - start)):
                x = jnp.where(group == n, moved(back[start + n], n - g), x)
            state_ref[some, start // groups, :] = x
    for r in range(-(-10 // groups), state_ref.shape[1]):
        state_ref[:, r, :] = jnp.zeros((count, 128), jnp.float32)


def plane_scan(reach_ref, blocks_ref, state_ref, map_ref, f_ref, b_ref):
    count = blocks_ref.shape[0]
    row = lax.broadcasted_iota(jnp.int32, (count, 128), 0)
    value = lambda n, some=slice(None): blocks_ref[some, n // 4, n % 4, :]
    v = [value(37 + n) for n in range(4)]
    below = jnp.where(row == 0, 0.0, pltpu.roll(v[3], 1, 0))
    above = jnp.where(row == count - 1, 0.0, pltpu.roll(v[0], count - 1, 0))
    here = blocks_ref[0, 10, 3:4, :]
    reach = reach_ref[0:1, :]
    for at in range(count):
        reach = jnp.where(here == float(at), reach_ref[at % 4 : at % 4 + 1, :], reach)
    inverse = -1.0 / reach
    for n, gradient in enumerate((0.5 * (v[1] - below), 0.5 * (above - v[2]))):
        map_ref[37 + n] = jnp.exp((1.0 + edge_slope * jnp.abs(gradient)) * inverse)
    for start in range(0, count, 8):
        some = slice(start, start + 8)
        block = unpack(lambda n: value(n, some))
        block = with_ends(block, map_ref[37, some, :], map_ref[38, some, :], value(41, some), value(42, some))
        for n, x in enumerate(pack(block)):
            map_ref[n, some, :] = x

    def block_at(m):
        return unpack(lambda n: map_ref[n, m : m + 1, :])

    f = [jnp.zeros((1, 128), jnp.float32)] * 4
    for m in range(count):
        for k in range(4):
            f_ref[k, m : m + 1, :] = f[k]
        f = forward_out(block_at(m), f)
    b = [jnp.zeros((1, 128), jnp.float32)] * 4
    for m in reversed(range(count)):
        for k in range(4):
            b_ref[k, m : m + 1, :] = b[k]
        b = backward_out(block_at(m), [f_ref[k, m : m + 1, :] for k in range(4)], b)

    here = jnp.broadcast_to(here, (4, 128))

    def mine(at):
        x = at(0)
        for g in range(1, count // 4):
            x = jnp.where(here > 4 * g - 0.5, at(g), x)
        return x

    for k in range(4):
        state_ref[:, k, :] = mine(lambda g: f_ref[k, 4 * g : 4 * g + 4, :])
        state_ref[:, 4 + k, :] = mine(lambda g: b_ref[k, 4 * g : 4 * g + 4, :])
    for n in range(2):
        state_ref[:, 8 + n, :] = mine(lambda g: map_ref[37 + n, 4 * g : 4 * g + 4, :])
    for n in range(10, 16):
        state_ref[:, n, :] = jnp.zeros((4, 128), jnp.float32)


f32 = lambda *shape: jax.ShapeDtypeStruct(shape, jnp.float32)
vmem = lambda *shape: pltpu.VMEM(shape, jnp.float32)
plane = (512, 128)


def call(kernel, out_shape, scratch, *operands):
    return pl.pallas_call(kernel, out_shape=out_shape, scratch_shapes=scratch, compiler_params=params)(*operands)


def states(chunks, axis):
    size = lax.axis_size(axis)
    groups = size // 4
    chunks = lax.all_to_all(chunks, axis, 0, 0, tiled=True)
    scratch = [vmem(37, 8, 128), vmem(4, 8, 128), vmem(4, 8, 128)]
    entering = call(functools.partial(line_scan, groups), f32(size, 16 // groups, 128), scratch, chunks)
    return lax.all_to_all(entering, axis, 0, 0, tiled=True)


def states_by_planes(chunks, axis, reach):
    size = lax.axis_size(axis)
    blocks = lax.all_to_all(chunks, axis, 0, 0, tiled=True)
    entering = call(plane_scan, f32(4, 16, 128), [vmem(39, size, 128), vmem(4, size, 128), vmem(4, size, 128)], reach, blocks)
    fours = [[4 * g + i for i in range(4)] for g in range(size // 4)]
    return lax.all_to_all(entering, axis, 0, 0, axis_index_groups=fours, tiled=True)


def per_device(intensity, reach_along_x, reach_along_y):
    def maps(axis):
        size = lax.axis_size(axis)
        return [f32(*padded), f32(37, 8, 128), f32(size, 11, 4, 128) if axis == "gy" else f32(size, SLOTS * 2 // size, 2, 128)]


    work = [vmem(SLOTS * APART, 128)]
    ending = [vmem(*padded), vmem(STEPS, 8, 128), vmem(*padded), vmem(8 * APART, 128)]
    vt, y_reach, source, dx, x_half, x_chunks = call(
        x_first, [f32(*plane), f32(4, 128), f32(*padded)] + maps("gx"), [vmem(4, 128)] + work,
        jnp.concatenate([intensity.reshape(plane), reach_along_x, reach_along_y]),
    )
    x_states = states(x_chunks, "gx")
    t, dy, y_half, y_chunks = call(
        x_second_y_first, [f32(*padded)] + maps("gy"), ending + work, vt, y_reach, source, dx, x_half, x_states
    )
    y_states = states_by_planes(y_chunks, "gy", y_reach)
    out = call(y_second, f32(*plane), ending, t, dy, y_half, y_states)
    return out.reshape(4, 128, 128)


def solution(mesh):
    return jax.shard_map(
        per_device,
        mesh=mesh,
        in_specs=(P(None, "gx", "gy"), P(None, "gy"), P(None, "gx")),
        out_specs=P(None, "gx", "gy"),
        check_vma=False,
    )
```
